32 devices in a mesh: dp: 4 (over y, x), mp: 8 (over z, core).
Axes of the slice: x: 2, y: 2, z: 4, core: 2. Of those that a mesh axis runs over, the one named last changes fastest.
Arguments:
- inputs: bfloat16 [32, 2560], P('dp'), may hold values from -6 to 6
- cotangent: bfloat16 [32, 2560], P('dp'), may hold values from -6 to 6
- w_in: bfloat16 [8, 16, 128, 128], P('mp', 'dp'), may hold values from -0.125 to 0.125
- w_out: bfloat16 [8, 16, 128, 128], P('mp', 'dp'), may hold values from -0.21875 to 0.21875
- block_index: int32 [8, 16], P('mp'), may hold values from 0 to 19, as said below
- block_count: int32 [8], P('mp'), may hold values from 8 to 16, as said below
- drop_seeds: int32 [32], P('dp'), may hold values from 0 to 1073741823
Outputs:
- outputs: bfloat16 [32, 2560], P(('dp', 'mp'))
- input_grad: bfloat16 [32, 2560], P(('dp', 'mp'))
- w_in_grad: float32 [8, 16, 128, 128], P('mp', 'dp')
- w_out_grad: float32 [8, 16, 128, 128], P('mp', 'dp')
The draws below stay inside these ranges and needn't reach their ends.
Inputs may be any that keep to these rules, and one draw needn't show every extreme that they name: `block_index`: each row holds 16 different feature blocks; the first slots hold a few shared blocks and the blocks of a butterfly over the feature blocks. `block_count`: some hidden block uses all 16 slots and some uses 16 // 2.
All inputs are finite; a program needn't handle non-finite values.
Results may differ from the reference program's by a relative error of at most 0.012.
Values may be sent and summed in bfloat16 or wider, within the bound.
No kernel may reach another device: no remote copies, remote signals or barrier semaphores. Data moves between devices by JAX's collectives and lax.ppermute only.
A program may use at most 64 MiB of HBM per device.

```python
import math
import jax
import jax.numpy as jnp
from jax import lax

D = 2560
BS = 128
K = 16
HBLOCKS = 8
TOK_G = 8
TOKENS = 32
N_DP = 4


def draw_block_index(key, part):
    block_cols = D // BS
    glob_count = max(1, block_cols // 10)
    fly_width = 2 ** int(math.floor(math.log2(block_cols - glob_count)))
    fly_levels = fly_width.bit_length() - 1
    column_order = jax.random.permutation(jax.random.fold_in(key, 1), block_cols).astype(jnp.int32)
    row_ids = jnp.arange(HBLOCKS, dtype=jnp.int32)
    fly_base = row_ids % fly_width
    column_ids = jnp.arange(block_cols, dtype=jnp.int32)
    priority = jnp.zeros((HBLOCKS, block_cols), jnp.int32)
    for glob_slot in range(glob_count):
        priority = priority | (column_ids[None, :] == column_order[glob_slot]).astype(jnp.int32)
    fly_cols = column_order[glob_count:glob_count + fly_width]
    priority = priority | (column_ids[None, :] == fly_cols[fly_base][:, None]).astype(jnp.int32)
    for fly_level in range(fly_levels):
        partner = fly_cols[fly_base ^ 1 << fly_level]
        priority = priority | (column_ids[None, :] == partner[:, None]).astype(jnp.int32)
    random_part = jax.random.randint(jax.random.fold_in(key, 2), (HBLOCKS, block_cols), 0, 1 << 20) * 64 + column_ids[None, :]
    sort_key = random_part - priority * (1 << 27)
    return jnp.argsort(sort_key, axis=1, stable=True)[:, :K].astype(jnp.int32)


def draw_block_count(key, part):
    counts = jax.random.randint(jax.random.fold_in(key, 3), (HBLOCKS,), K // 2, K + 1).astype(jnp.int32)
    first_pos = jax.random.randint(jax.random.fold_in(key, 4), (), 0, HBLOCKS)
    second_pos = (first_pos + 1 + jax.random.randint(jax.random.fold_in(key, 5), (), 0, HBLOCKS - 1)) % HBLOCKS
    return counts.at[first_pos].set(K).at[second_pos].set(K // 2).astype(jnp.int32)


def with_ends(values, own_key, least, high):
    longest = values.shape.index(max(values.shape))
    spots = []
    for shift in (0, 1):
        where = [jax.random.randint(jax.random.fold_in(own_key, axis), (), 0, length) for axis, length in enumerate(values.shape)]
        where[longest] = (where[longest] + shift) % values.shape[longest]
        spots.append(tuple(where))
    return values.at[spots[0]].set(least).at[spots[1]].set(high)


def levels(key, dims, shards, smallest, top_value):
    def one(dim, parts):
        steps = jax.random.uniform(jax.random.fold_in(jax.random.fold_in(key, 6), dim), (parts,), jnp.float32, smallest / len(shards), top_value / len(shards))
        return jnp.repeat(jnp.exp(steps), dims[dim] // parts).reshape((-1,) + (1,) * (len(dims) - dim - 1))

    level = one(*shards[0])
    for cut in shards[1:]:
        level = level * one(*cut)
    return level


def scatter_about(rng, extent, deviation, most, shards=(), held_as=jnp.bfloat16):
    values = jax.random.normal(rng, extent, jnp.float32) * deviation
    if len(shards) > 0:
        values = levels(rng, extent, shards, -0.22, 0.18) * values
    return jnp.clip(values, min=-most, max=most).astype(held_as)


def setup_inputs(seed: int = 0) -> dict:
    keys = jax.random.split(jax.random.key(seed), 8)
    return {
        "inputs": scatter_about(keys[0], (TOKENS, D), 1.0, 6.0, ((0, 4),)),
        "cotangent": scatter_about(keys[1], (TOKENS, D), 1.0, 6.0, ((0, 4),)),
        "w_in": scatter_about(keys[2], (HBLOCKS, K, BS, BS), (BS * K) ** -0.5, 0.125, ((0, 8), (1, 4))),
        "w_out": scatter_about(keys[3], (HBLOCKS, K, BS, BS), (BS * K * HBLOCKS // (D // BS)) ** -0.5, 0.21875, ((0, 8), (1, 4))),
        "block_index": draw_block_index(jax.random.fold_in(keys[7], 71), 0),
        "block_count": draw_block_count(jax.random.fold_in(keys[7], 71), 0),
        "drop_seeds": with_ends(jax.random.randint(keys[6], (TOKENS,), 0, 1073741824), jax.random.fold_in(keys[6], 1), 0, 1073741823).astype(jnp.int32),
    }


def scramble(value):
    value = value ^ lax.shift_right_logical(value, jnp.int32(16))
    value = value * jnp.int32(73244475)
    value = value ^ lax.shift_right_logical(value, jnp.int32(16))
    value = value * jnp.int32(73244475)
    value = value ^ lax.shift_right_logical(value, jnp.int32(16))
    return value

def keep_factor(seeds, first_unit):
    units = first_unit + jnp.arange(BS, dtype=jnp.int32)
    mixed = scramble(seeds[:, None] + units[None, :] * jnp.int32(668265261))
    kept = mixed & jnp.int32(7) != jnp.int32(0)
    return kept.astype(jnp.float32) * jnp.float32(8.0 / 7.0)

def gelu_parts(pre_act):
    coeff = math.sqrt(2.0 / math.pi)
    inner = coeff * (pre_act + 0.044715 * pre_act ** 3)
    tanh_val = jnp.tanh(inner)
    activation = 0.5 * pre_act * (1.0 + tanh_val)
    slope = 0.5 * (1.0 + tanh_val) + 0.5 * pre_act * (1.0 - tanh_val * tanh_val) * coeff * (1.0 + 3.0 * 0.044715 * pre_act * pre_act)
    return (activation, slope)

def round_half(value):
    return lax.optimization_barrier(value.astype(jnp.bfloat16)).astype(jnp.float32)

def reference(inputs, cotangent, w_in, w_out, block_index, block_count, drop_seeds):
    block_cols = D // BS
    tok_blocks = inputs.reshape(TOKENS, block_cols, BS)
    cot_blocks = cotangent.reshape(TOKENS, block_cols, BS)
    slot_ids = jnp.arange(K, dtype=jnp.int32)
    col_ids = jnp.arange(block_cols, dtype=jnp.int32)

    def one_block(carry, item):
        out_acc, in_acc = carry
        hidden_id, idx_row, count, w_first, w_second = item
        valid = (slot_ids < count).astype(jnp.bfloat16)
        w1m = (w_first * valid[:, None, None]).astype(jnp.float32)
        w2m = (w_second * valid[:, None, None]).astype(jnp.float32)
        selected = jnp.take(tok_blocks, idx_row, axis=1).astype(jnp.float32)
        cot_sel = jnp.take(cot_blocks, idx_row, axis=1).astype(jnp.float32)
        pre_act = jnp.einsum('tkc,kcf->tf', selected, w1m)
        activation, slope = gelu_parts(pre_act)
        keep_scale = keep_factor(drop_seeds, hidden_id * BS)
        dropped = (activation * keep_scale).astype(jnp.bfloat16)
        one_hot = (idx_row[:, None] == col_ids[None, :]).astype(jnp.float32)
        out_blocks = jnp.einsum('tf,kfc->tkc', dropped.astype(jnp.float32), w2m)
        out_term = jnp.einsum('tkc,kd->tdc', out_blocks, one_hot).reshape(TOKENS, D)
        out_acc = out_acc + out_term
        grad_drop = jnp.einsum('tkc,kfc->tf', cot_sel, w2m)
        grad_pre = (grad_drop * keep_scale * slope).astype(jnp.bfloat16)
        in_blocks = jnp.einsum('tf,kcf->tkc', grad_pre.astype(jnp.float32), w1m)
        in_term = jnp.einsum('tkc,kd->tdc', in_blocks, one_hot).reshape(TOKENS, D)
        in_acc = in_acc + in_term
        valid_full = valid.astype(jnp.float32)
        group_sel = selected.reshape(N_DP, TOK_G, K, BS)
        group_cot = cot_sel.reshape(N_DP, TOK_G, K, BS)
        group_pre = grad_pre.astype(jnp.float32).reshape(N_DP, TOK_G, BS)
        group_drop = dropped.astype(jnp.float32).reshape(N_DP, TOK_G, BS)
        term_in = jnp.einsum('gtkc,gtf->gkcf', group_sel, group_pre) * valid_full[None, :, None, None]
        term_out = jnp.einsum('gtf,gtkc->gkfc', group_drop, group_cot) * valid_full[None, :, None, None]
        term_in = round_half(term_in)
        term_out = round_half(term_out)
        return ((out_acc, in_acc), (lax.optimization_barrier(jnp.sum(term_in, axis=0)), lax.optimization_barrier(jnp.sum(term_out, axis=0))))
    start = (jnp.zeros((TOKENS, D), jnp.float32), jnp.zeros((TOKENS, D), jnp.float32))
    hidden_ids = jnp.arange(HBLOCKS, dtype=jnp.int32)
    (out_acc, in_acc), (grad_in, grad_out) = lax.scan(one_block, start, (hidden_ids, block_index, block_count, w_in, w_out))
    return (out_acc.astype(jnp.bfloat16), in_acc.astype(jnp.bfloat16), grad_in, grad_out)
```

```python
import functools
import math

import jax
import jax.numpy as jnp
from jax import lax
from jax.experimental import pallas as pl
from jax.experimental.pallas import tpu as pltpu
from jax.sharding import Mesh, PartitionSpec as P

BS = 128
F32 = jnp.float32
BF16 = jnp.bfloat16
VMEM_LIMIT = 48 * 2**20


def scramble(value):
    value = value ^ lax.shift_right_logical(value, jnp.int32(16))
    value = value * jnp.int32(73244475)
    value = value ^ lax.shift_right_logical(value, jnp.int32(16))
    value = value * jnp.int32(73244475)
    value = value ^ lax.shift_right_logical(value, jnp.int32(16))
    return value


def keep_factor(seeds, first_unit):
    units = first_unit + jnp.arange(BS, dtype=jnp.int32)
    mixed = scramble(seeds[:, None] + units[None, :] * jnp.int32(668265261))
    kept = mixed & jnp.int32(7) != jnp.int32(0)
    return kept.astype(F32) * jnp.float32(8.0 / 7.0)


def gelu_parts(pre_act):
    coeff = math.sqrt(2.0 / math.pi)
    inner = coeff * (pre_act + 0.044715 * pre_act**3)
    tanh_val = jnp.tanh(inner)
    activation = 0.5 * pre_act * (1.0 + tanh_val)
    slope = 0.5 * (1.0 + tanh_val) + 0.5 * pre_act * (1.0 - tanh_val * tanh_val) * coeff * (
        1.0 + 3.0 * 0.044715 * pre_act * pre_act
    )
    return (activation, slope)


def dot(left, right, dims):
    return lax.dot_general(left, right, (dims, ((), ())), preferred_element_type=F32)


def feature_block(pieces, index, used):
    at = pl.ds(pl.multiple_of(index * BS, BS), BS)
    rows = [piece[:, at].astype(F32) for piece in pieces]
    return (jnp.concatenate(rows, axis=0) * used).astype(BF16)


def slot(meta, which, slots):
    return meta[which], meta[2 * slots + which].astype(F32)


def partial_kernel(groups, slots, meta, *refs):
    toks, cots = refs[:groups], refs[groups : 2 * groups]
    keep, w1_own, w1_far, w2_own, w2_far, out = refs[2 * groups :]
    tokens = groups * toks[0].shape[0]
    pre = jnp.zeros((tokens, BS), F32)
    grad = jnp.zeros((tokens, BS), F32)
    for side, w1, w2 in ((0, w1_own, w2_own), (1, w1_far, w2_far)):
        for j in range(slots):
            index, used = slot(meta, side * slots + j, slots)
            pre += dot(feature_block(toks, index, used), w1[0, j], ((1,), (0,)))
            grad += dot(feature_block(cots, index, used), w2[0, j], ((1,), (1,)))
    out[:tokens] = pre
    out[tokens : 2 * tokens] = grad
    out[2 * tokens :] = keep[...]


def swap_halves(value):
    half = value.shape[0] // 2
    return jnp.concatenate([value[half:], value[:half]], axis=0)


def hidden_kernel(groups, slots, blocks, meta, *refs):
    toks, cots = refs[:groups], refs[groups : 2 * groups]
    mine, theirs, w1_own, w1_far, w2_own, w2_far, away, home, rows_far, rows_own, acc = refs[2 * groups :]
    tokens = groups * toks[0].shape[0]
    half = tokens // 2
    acc[...] = jnp.zeros_like(acc)
    pre = mine[:tokens] + swap_halves(theirs[:tokens])
    grad = mine[tokens : 2 * tokens] + swap_halves(theirs[tokens : 2 * tokens])
    keep = jnp.concatenate([mine[2 * tokens :], theirs[2 * tokens :]], axis=0)
    activation, slope = gelu_parts(pre)
    dropped = (activation * keep).astype(BF16)
    grad_pre = (grad * keep * slope).astype(BF16)
    for side, w1, w2 in ((0, w1_own, w2_own), (1, w1_far, w2_far)):
        for j in range(slots):
            index, used = slot(meta, side * slots + j, slots)
            out_block = dot(dropped, w2[0, j], ((1,), (0,))) * used
            in_block = dot(grad_pre, w1[0, j], ((1,), (1,))) * used
            acc[:, pl.ds(index, 1), :] = out_block.reshape(tokens, 1, BS)
            acc[:, pl.ds(blocks + index, 1), :] = in_block.reshape(tokens, 1, BS)
    away[...] = acc[half:].astype(BF16)
    home[...] = acc[:half]
    for side, rows in ((0, rows_own), (1, rows_far)):
        rows[:, :BS] = dropped
        rows[:, BS : 2 * BS] = grad_pre
        for j in range(slots):
            index, used = slot(meta, side * slots + j, slots)
            rows[:, (2 + j) * BS : (3 + j) * BS] = feature_block(toks, index, used)
            at = 2 + slots + j
            rows[:, at * BS : (at + 1) * BS] = feature_block(cots, index, used)


def grad_kernel(slots, own, far, grad_in, grad_out):
    def column(at):
        cut = slice(at * BS, (at + 1) * BS)
        return jnp.concatenate([own[:, cut], far[:, cut]], axis=0)

    dropped, grad_pre = column(0), column(1)
    for j in range(slots):
        grad_in[0, j] = dot(column(2 + j), grad_pre, ((0,), (0,)))
        grad_out[0, j] = dot(dropped, column(2 + slots + j), ((0,), (0,)))


def call(kernel, n_vmem, out_shape, flops, nbytes, scalars=True, scratch=()):
    vmem = pl.BlockSpec(memory_space=pltpu.VMEM)
    head = [pl.BlockSpec(memory_space=pltpu.SMEM)] if scalars else []
    return pl.pallas_call(
        kernel,
        out_shape=out_shape,
        in_specs=head + [vmem] * n_vmem,
        out_specs=jax.tree.map(lambda _: vmem, out_shape),
        scratch_shapes=list(scratch),
        compiler_params=pltpu.CompilerParams(vmem_limit_bytes=VMEM_LIMIT),
        cost_estimate=pl.CostEstimate(flops=flops, bytes_accessed=nbytes, transcendentals=0),
    )


def flip(value, axis, size, bit):
    return lax.ppermute(value, axis, [(i, i ^ bit) for i in range(size)])


def body(n_dy, n_mp, inputs, cotangent, w_in, w_out, block_index, block_count, drop_seeds):
    local, width = inputs.shape
    blocks = width // BS
    slots = w_in.shape[1]
    tokens = n_dy * local
    rank = lax.axis_index("mp")
    dx = lax.axis_index("dx")
    first = (lax.axis_index("dy") * 2 + dx) * slots

    w1_far = flip(w_in, "dx", 2, 1)
    w2_far = flip(w_out, "dx", 2, 1)
    toks, cots = [inputs], [cotangent]
    bit = 1
    while bit < n_dy:
        toks += [flip(piece, "dy", n_dy, bit) for piece in toks]
        cots += [flip(piece, "dy", n_dy, bit) for piece in cots]
        bit *= 2

    own_slots = first + jnp.arange(slots, dtype=jnp.int32)
    far_slots = own_slots + (1 - 2 * dx) * slots
    both = jnp.concatenate([own_slots, far_slots])
    used = (both < block_count[0]).astype(jnp.int32)
    meta = jnp.concatenate([block_index[0][both], used])
    keep = keep_factor(drop_seeds, rank * BS)

    shape = jax.ShapeDtypeStruct
    work = 2 * tokens * 2 * slots * 2 * BS * BS
    moved = 4 * slots * BS * BS * 2
    mine = call(
        functools.partial(partial_kernel, n_dy, slots),
        2 * n_dy + 5,
        shape((2 * tokens + local, BS), F32),
        work,
        moved,
    )(meta, *toks, *cots, keep, w_in, w1_far, w_out, w2_far)

    bit = 1
    while bit < n_dy:
        theirs = flip(mine, "dy", n_dy, bit)
        if 2 * bit < n_dy:

            def swapped(value):
                parts = value.reshape(n_dy // (2 * bit), 2, bit * local, BS)
                return parts[:, ::-1].reshape(tokens, BS)

            mine = jnp.concatenate(
                [
                    mine[:tokens] + swapped(theirs[:tokens]),
                    mine[tokens : 2 * tokens] + swapped(theirs[tokens : 2 * tokens]),
                    mine[2 * tokens :],
                    theirs[2 * tokens :],
                ]
            )
        bit *= 2

    half = tokens // 2
    away, total, rows_far, rows_own = call(
        functools.partial(hidden_kernel, n_dy, slots, blocks),
        2 * n_dy + 6,
        (
            shape((half, 2 * blocks, BS), BF16),
            shape((half, 2 * blocks, BS), F32),
            shape((tokens, (2 + 2 * slots) * BS), BF16),
            shape((tokens, (2 + 2 * slots) * BS), BF16),
        ),
        work,
        moved,
        scratch=[pltpu.VMEM((tokens, 2 * blocks, BS), F32)],
    )(meta, *toks, *cots, mine, theirs, w_in, w1_far, w_out, w2_far)

    bit = n_dy // 2
    total = total + flip(away, "dy", n_dy, bit).astype(F32)
    while bit > 1:
        bit //= 2
        cut = bit * local
        total = total[:cut] + flip(total[cut:].astype(BF16), "dy", n_dy, bit).astype(F32)

    rows_got = flip(rows_far, "dx", 2, 1)
    grad_in, grad_out = call(
        functools.partial(grad_kernel, slots),
        2,
        (shape((1, slots, BS, BS), F32), shape((1, slots, BS, BS), F32)),
        4 * tokens * slots * 2 * BS * BS,
        2 * slots * BS * BS * 4,
        scalars=False,
    )(rows_own, rows_got)

    bit = 1
    while bit < n_mp:
        mine_bit = (rank // bit) % 2
        pairs = total.reshape(total.shape[0] // 2, 2, 2 * blocks, BS)
        away = lax.dynamic_index_in_dim(pairs, 1 - mine_bit, 1, keepdims=False)
        total = lax.dynamic_index_in_dim(pairs, mine_bit, 1, keepdims=False)
        sent = F32 if bit == 1 else BF16
        total = total + flip(away.astype(sent), "mp", n_mp, bit).astype(F32)
        bit *= 2
    total = total.astype(BF16)
    rows = total.shape[0]
    outputs = total[:, :blocks].reshape(rows, width)
    input_grad = total[:, blocks:].reshape(rows, width)
    return (outputs, input_grad, grad_in, grad_out)


def solution(mesh):
    n_dp, n_mp = mesh.shape["dp"], mesh.shape["mp"]
    fine = Mesh(mesh.devices.reshape(n_dp // 2, 2, n_mp), ("dy", "dx", "mp"))
    dp = ("dy", "dx")
    placed = (
        P(dp, None),
        P(dp, None),
        P("mp", dp, None, None),
        P("mp", dp, None, None),
        P("mp", None),
        P("mp"),
        P(dp),
    )
    return jax.shard_map(
        functools.partial(body, n_dp // 2, n_mp),
        mesh=fine,
        in_specs=placed,
        out_specs=(
            P(("dy", "dx", "mp"), None),
            P(("dy", "dx", "mp"), None),
            P("mp", dp, None, None),
            P("mp", dp, None, None),
        ),
        check_vma=False,
    )
```

```python
import functools
import math

import jax
import jax.numpy as jnp
from jax import lax
from jax.experimental import pallas as pl
from jax.experimental.pallas import tpu as pltpu
from jax.sharding import PartitionSpec as P

BS = 128
F32 = jnp.float32
BF16 = jnp.bfloat16
VMEM_LIMIT = 48 * 2**20


def scramble(value):
    value = value ^ lax.shift_right_logical(value, jnp.int32(16))
    value = value * jnp.int32(73244475)
    value = value ^ lax.shift_right_logical(value, jnp.int32(16))
    value = value * jnp.int32(73244475)
    value = value ^ lax.shift_right_logical(value, jnp.int32(16))
    return value


def keep_factor(seeds, first_unit):
    units = first_unit + jnp.arange(BS, dtype=jnp.int32)
    mixed = scramble(seeds[:, None] + units[None, :] * jnp.int32(668265261))
    kept = mixed & jnp.int32(7) != jnp.int32(0)
    return kept.astype(F32) * jnp.float32(8.0 / 7.0)


def gelu_parts(pre_act):
    coeff = math.sqrt(2.0 / math.pi)
    inner = coeff * (pre_act + 0.044715 * pre_act**3)
    tanh_val = jnp.tanh(inner)
    activation = 0.5 * pre_act * (1.0 + tanh_val)
    slope = 0.5 * (1.0 + tanh_val) + 0.5 * pre_act * (1.0 - tanh_val * tanh_val) * coeff * (
        1.0 + 3.0 * 0.044715 * pre_act * pre_act
    )
    return (activation, slope)


def dot(left, right, dims):
    return lax.dot_general(left, right, (dims, ((), ())), preferred_element_type=F32)


def slot(block_index, block_count, first, at):
    number = first ^ at
    return block_index[0, number], (number < block_count[0]).astype(F32)


def block_of(picks, half, place):
    local = picks.shape[0] // 2
    rows = picks[:, place * BS : (place + 1) * BS].astype(F32)
    return rows[half * local : (half + 1) * local].astype(BF16)


def add_slots(slots, picks, pre, grad, masks_in, masks_out, weights):
    firsts, seconds = weights[: len(masks_in)], weights[len(masks_in) :]
    for mask, first in zip(masks_in, firsts):
        for j in range(slots):
            pre += dot(block_of(picks, 0, mask * slots + j), first[0, j], ((1,), (0,)))
    for mask, second in zip(masks_out, seconds):
        for j in range(slots):
            grad += dot(block_of(picks, 1, mask * slots + j), second[0, j], ((1,), (1,)))
    return pre, grad


def select_kernel(slots, masks_in, masks_out, block_index, block_count, tokens, *refs):
    *weights, picks, table, sums = refs
    first = lax.axis_index("dp") * slots
    local = sums.shape[0] // 2
    row = lax.broadcasted_iota(jnp.int32, table.shape, 0)
    lane = lax.broadcasted_iota(jnp.int32, table.shape, 1)
    entries = jnp.zeros(table.shape, jnp.int32)
    for place in range(picks.shape[1] // BS):
        index, used = slot(block_index, block_count, first, place)
        at = pl.ds(pl.multiple_of(index * BS, BS), BS)
        picks[:, place * BS : (place + 1) * BS] = (tokens[:, at].astype(F32) * used).astype(BF16)
        entry = jnp.where(row == 0, index, used.astype(jnp.int32))
        entries = jnp.where(lane == place, entry, entries)
    table[...] = entries
    zero = jnp.zeros((local, BS), F32)
    pre, grad = add_slots(slots, picks, zero, zero, masks_in, masks_out, weights)
    sums[:local] = pre
    sums[local:] = grad


def hold_kernel(first, second, held_first, held_second, sems):
    copies = [
        pltpu.make_async_copy(first, held_first, sems.at[0]),
        pltpu.make_async_copy(second, held_second, sems.at[1]),
    ]
    for copy in copies:
        copy.start()
    for copy in copies:
        copy.wait()


def partial_kernel(slots, masks_in, masks_out, picks, *refs):
    *weights, sums, out = refs
    local = picks.shape[0] // 2
    pre, grad = add_slots(slots, picks, sums[:local], sums[local:], masks_in, masks_out, weights)
    out[:local] = pre
    out[local:] = grad


def hidden_kernel(slots, blocks, masks_in, masks_out, late, picks, table, keep, sums, *refs):
    count = len(masks_in)
    firsts = dict(zip(masks_in, refs[:count]))
    seconds = dict(zip(masks_out, refs[count : 2 * count]))
    away, home, *rows = refs[2 * count : -1]
    acc = refs[-1]
    local = keep.shape[0]
    half = local // 2
    odd = lax.axis_index("mp") % 2
    acc[...] = jnp.zeros_like(acc)
    entries = table[...]
    pre, grad = add_slots(
        slots, picks, sums[:local], sums[local:], late, late, [firsts[m] for m in late] + [seconds[m] for m in late]
    )
    activation, slope = gelu_parts(pre)
    dropped_full = activation * keep[...]
    grad_full = grad * keep[...] * slope
    dropped, grad_pre = dropped_full.astype(BF16), grad_full.astype(BF16)
    for mask in range(count):
        for j in range(slots):
            at = mask * slots + j
            index, used = entries[0, at], entries[1, at].astype(F32)
            out_block = dot(dropped, seconds[mask][0, j], ((1,), (0,))) * used
            in_block = dot(grad_pre, firsts[mask][0, j], ((1,), (1,))) * used
            acc[:, :, pl.ds(index, 1), :] = out_block.reshape(half, 2, 1, BS)
            acc[:, :, pl.ds(blocks + index, 1), :] = in_block.reshape(half, 2, 1, BS)
    even_rows, odd_rows = acc[:, 0], acc[:, 1]
    away[...] = jnp.where(odd == 1, even_rows, odd_rows).astype(BF16)
    home[...] = jnp.where(odd == 1, odd_rows, even_rows)
    hidden = jnp.concatenate([dropped_full, grad_full], axis=0).astype(BF16)
    for mask, message in enumerate(rows):
        message[:, :BS] = hidden
        message[:, BS:] = picks[:, mask * slots * BS : (mask + 1) * slots * BS]


def all_rows(messages, half, place):
    return jnp.concatenate([block_of(message, half, place) for message in messages], axis=0)


def grad_kernel(slots, *refs):
    *messages, grad_in, grad_out, order = refs
    order[...] = jnp.zeros_like(order)
    dropped, grad_pre = all_rows(messages, 0, 0), all_rows(messages, 1, 0)
    for j in range(slots):
        grad_in[0, j] = dot(all_rows(messages, 0, 1 + j), grad_pre, ((0,), (0,)))
        grad_out[0, j] = dot(dropped, all_rows(messages, 1, 1 + j), ((0,), (0,)))


def last_kernel(blocks, kept, got, order, outputs, input_grad):
    for row in range(kept.shape[0]):
        total = kept[row] + got[row].astype(F32)
        for result, start in ((outputs, 0), (input_grad, blocks)):
            line = [total[start + i : start + i + 1] for i in range(blocks)]
            result[row : row + 1] = jnp.concatenate(line, axis=1).astype(BF16)


def call(kernel, n_vmem, out_shape, flops, nbytes, scalars=0, scratch=()):
    vmem = pl.BlockSpec(memory_space=pltpu.VMEM)
    head = [pl.BlockSpec(memory_space=pltpu.SMEM)] * scalars
    return pl.pallas_call(
        kernel,
        out_shape=out_shape,
        in_specs=head + [vmem] * n_vmem,
        out_specs=jax.tree.map(lambda _: vmem, out_shape),
        scratch_shapes=list(scratch),
        compiler_params=pltpu.CompilerParams(vmem_limit_bytes=VMEM_LIMIT),
        cost_estimate=pl.CostEstimate(flops=flops, bytes_accessed=nbytes, transcendentals=0),
    )


def flip(value, axis, size, mask):
    return lax.ppermute(value, axis, [(i, i ^ mask) for i in range(size)]) if mask else value


def gather(values, held, n_dp, orders):
    pieces = [{0: value} for value in values]
    for step, bits in enumerate(zip(*orders)):
        pieces = [
            {**parts, **{mask | bit: flip(part, "dp", n_dp, bit) for mask, part in parts.items()}}
            for parts, bit in zip(pieces, bits)
        ]
        if step == 0:
            for parts, own in zip(pieces, held):
                parts[0] = own
    return pieces


def exchange(messages, n_dp, bits):
    for bit in bits:
        size = messages[0].shape[1]
        leaving = jnp.concatenate([message for mask, message in enumerate(messages) if mask & bit], axis=1)
        arrived = flip(leaving, "dp", n_dp, bit)
        place = 0
        for mask in range(len(messages)):
            if mask & bit:
                messages[mask] = arrived[:, place * size : (place + 1) * size]
                place += 1
    return messages


def body(n_dp, n_mp, inputs, cotangent, w_in, w_out, block_index, block_count, drop_seeds):
    local, width = inputs.shape
    blocks = width // BS
    slots = w_in.shape[1]
    shape = jax.ShapeDtypeStruct
    piece_flops = 2 * local * slots * BS * BS
    piece_bytes = slots * BS * BS * 2

    bits = [1 << i for i in range(n_dp.bit_length() - 1)]
    held = pl.pallas_call(
        hold_kernel,
        out_shape=[shape(w_in.shape, BF16), shape(w_out.shape, BF16)],
        in_specs=[pl.BlockSpec(memory_space=pl.ANY)] * 2,
        out_specs=[pl.BlockSpec(memory_space=pltpu.VMEM)] * 2,
        scratch_shapes=[pltpu.SemaphoreType.DMA((2,))],
    )(w_in, w_out)
    firsts, seconds = gather([w_in, w_out], held, n_dp, [bits, bits[::-1]])

    rank = lax.axis_index("mp")
    keep = keep_factor(drop_seeds, rank * BS)
    steps = [([0, bits[0]], [0, bits[-1]])]
    late = [n_dp - 1]
    steps.append([[mask for mask in range(n_dp - 1) if mask not in done] for done in steps[0]])
    weights = [[firsts[m] for m in masks_in] + [seconds[m] for m in masks_out] for masks_in, masks_out in steps]
    picks, table, sums = call(
        functools.partial(select_kernel, slots, *steps[0]),
        1 + len(weights[0]),
        [
            shape((2 * local, n_dp * slots * BS), BF16),
            shape((8, BS), jnp.int32),
            shape((2 * local, BS), F32),
        ],
        0,
        0,
        scalars=2,
    )(block_index, block_count, jnp.concatenate([inputs, cotangent]), *weights[0])
    sums = call(
        functools.partial(partial_kernel, slots, *steps[1]),
        2 + len(weights[1]),
        shape((2 * local, BS), F32),
        0,
        0,
    )(picks, *weights[1], sums)

    half = local // 2
    masks_in, masks_out = sorted(firsts), sorted(seconds)
    away, home, *rows = call(
        functools.partial(hidden_kernel, slots, blocks, masks_in, masks_out, late),
        4 + 2 * n_dp,
        [shape((half, 2 * blocks, BS), BF16), shape((half, 2 * blocks, BS), F32)]
        + [shape((2 * local, (1 + slots) * BS), BF16)] * n_dp,
        (2 * n_dp + 2) * piece_flops,
        2 * n_dp * piece_bytes,
        scratch=[pltpu.VMEM((half, 2, 2 * blocks, BS), F32)],
    )(picks, table, keep, sums, *[firsts[m] for m in masks_in], *[seconds[m] for m in masks_out])

    total = home + flip(away, "mp", n_mp, 1).astype(F32)
    messages = exchange(rows, n_dp, bits)
    bit = 2
    while bit < n_mp:
        mine_bit = (rank // bit) % 2
        pairs = total.reshape(total.shape[0] // 2, 2, 2 * blocks, BS)
        away = lax.dynamic_index_in_dim(pairs, 1 - mine_bit, 1, keepdims=False)
        home = lax.dynamic_index_in_dim(pairs, mine_bit, 1, keepdims=False)
        got = flip(away.astype(BF16), "mp", n_mp, bit)
        total = home + got.astype(F32)
        bit *= 2

    grad_shape = shape((1, slots, BS, BS), F32)
    grad_in, grad_out, order = call(
        functools.partial(grad_kernel, slots),
        n_dp,
        [grad_shape, grad_shape, shape((8, BS), F32)],
        2 * n_dp * piece_flops,
        4 * piece_bytes,
    )(*messages)
    done = home.shape[0]
    outputs, input_grad = call(
        functools.partial(last_kernel, blocks),
        3,
        [shape((done, width), BF16), shape((done, width), BF16)],
        done * 2 * width,
        done * 2 * width * 8,
    )(home, got, order)
    return (outputs, input_grad, grad_in, grad_out)


def solution(mesh):
    placed = (
        P("dp", None),
        P("dp", None),
        P("mp", "dp", None, None),
        P("mp", "dp", None, None),
        P("mp", None),
        P("mp"),
        P("dp"),
    )
    return jax.shard_map(
        functools.partial(body, mesh.shape["dp"], mesh.shape["mp"]),
        mesh=mesh,
        in_specs=placed,
        out_specs=(
            P(("dp", "mp"), None),
            P(("dp", "mp"), None),
            P("mp", "dp", None, None),
            P("mp", "dp", None, None),
        ),
        check_vma=False,
    )
```

```python
import functools
import math

import jax
import jax.numpy as jnp
from jax import lax
from jax.experimental import pallas as pl
from jax.experimental.pallas import tpu as pltpu
from jax.sharding import PartitionSpec as P

BS = 128
F32 = jnp.float32
BF16 = jnp.bfloat16
VMEM_LIMIT = 48 * 2**20


def scramble(value):
    value = value ^ lax.shift_right_logical(value, jnp.int32(16))
    value = value * jnp.int32(73244475)
    value = value ^ lax.shift_right_logical(value, jnp.int32(16))
    value = value * jnp.int32(73244475)
    value = value ^ lax.shift_right_logical(value, jnp.int32(16))
    return value


def keep_factor(seeds, first_unit):
    units = first_unit + jnp.arange(BS, dtype=jnp.int32)
    mixed = scramble(seeds[:, None] + units[None, :] * jnp.int32(668265261))
    kept = mixed & jnp.int32(7) != jnp.int32(0)
    return kept.astype(F32) * jnp.float32(8.0 / 7.0)


def gelu_parts(pre_act):
    coeff = math.sqrt(2.0 / math.pi)
    inner = coeff * (pre_act + 0.044715 * pre_act**3)
    tanh_val = jnp.tanh(inner)
    activation = 0.5 * pre_act * (1.0 + tanh_val)
    slope = 0.5 * (1.0 + tanh_val) + 0.5 * pre_act * (1.0 - tanh_val * tanh_val) * coeff * (
        1.0 + 3.0 * 0.044715 * pre_act * pre_act
    )
    return (activation, slope)


def dot(left, right, dims):
    return lax.dot_general(left, right, (dims, ((), ())), preferred_element_type=F32)


def slot(listed, count, first, at):
    number = first ^ at
    return listed[number], (number < listed[count]).astype(F32)


def block_of(picks, half, place):
    local = picks.shape[0] // 2
    rows = picks[:, place * BS : (place + 1) * BS].astype(F32)
    return rows[half * local : (half + 1) * local].astype(BF16)


def side_by_side(weights, slots):
    return jnp.concatenate([weights[0, j] for j in range(slots)], axis=1)


def stacked(weights, slots):
    return weights[0].reshape(slots * BS, BS)


def add_slots(slots, picks, pre, grad, masks_in, masks_out, firsts, seconds):
    local = picks.shape[0] // 2
    span = slots * BS
    for mask, first in zip(masks_in, firsts):
        rows = picks[:, mask * span : (mask + 1) * span].astype(F32)[:local].astype(BF16)
        pre += dot(rows, stacked(first, slots), ((1,), (0,)))
    for mask, second in zip(masks_out, seconds):
        rows = picks[:, mask * span : (mask + 1) * span].astype(F32)[local:].astype(BF16)
        grad += dot(rows, side_by_side(second, slots), ((1,), (1,)))
    return pre, grad


def select_kernel(slots, masks_in, masks_out, listed, tokens, *refs):
    *weights, picks, table, sums = refs
    first = lax.axis_index("dp") * slots
    local = sums.shape[0] // 2
    row = lax.broadcasted_iota(jnp.int32, table.shape, 0)
    lane = lax.broadcasted_iota(jnp.int32, table.shape, 1)
    entries = jnp.zeros(table.shape, jnp.int32)
    count = picks.shape[1] // BS
    for place in range(count):
        index, used = slot(listed, count, first, place)
        at = pl.ds(pl.multiple_of(index * BS, BS), BS)
        picks[:, place * BS : (place + 1) * BS] = (tokens[:, at].astype(F32) * used).astype(BF16)
        entry = jnp.where(row == 0, index, used.astype(jnp.int32))
        entries = jnp.where(lane == place, entry, entries)
    table[...] = entries
    zero = jnp.zeros((local, BS), F32)
    firsts, seconds = weights[: len(masks_in)], weights[len(masks_in) :]
    pre, grad = add_slots(slots, picks, zero, zero, masks_in, masks_out, firsts, seconds)
    sums[:local] = pre
    sums[local:] = grad


def partial_kernel(slots, masks_in, masks_out, picks, *refs):
    *weights, sums, out = refs
    local = picks.shape[0] // 2
    seconds, firsts = weights[: len(masks_out)], weights[len(masks_out) :]
    pre, grad = add_slots(slots, picks, sums[:local], sums[local:], masks_in, masks_out, firsts, seconds)
    out[:local] = pre
    out[local:] = grad


def hidden_kernel(slots, blocks, masks_in, masks_out, late, picks, table, keep, sums, *refs):
    count = len(masks_in)
    firsts = dict(zip(masks_in, refs[:count]))
    seconds = dict(zip(masks_out, refs[count : 2 * count]))
    away, home, *rows = refs[2 * count : -1]
    acc = refs[-1]
    local = keep.shape[0]
    half = local // 2
    odd = lax.axis_index("mp") % 2
    acc[...] = jnp.zeros_like(acc)
    entries = table[...]
    pre, grad = add_slots(
        slots, picks, sums[:local], sums[local:], late, late, [firsts[m] for m in late], [seconds[m] for m in late]
    )
    activation, slope = gelu_parts(pre)
    dropped_full = activation * keep[...]
    grad_full = grad * keep[...] * slope
    dropped, grad_pre = dropped_full.astype(BF16), grad_full.astype(BF16)
    for mask in range(count):
        out_row = dot(dropped, side_by_side(seconds[mask], slots), ((1,), (0,)))
        in_row = dot(grad_pre, stacked(firsts[mask], slots), ((1,), (1,)))
        for j in range(slots):
            at = mask * slots + j
            index, used = entries[0, at], entries[1, at].astype(F32)
            cut = slice(j * BS, (j + 1) * BS)
            acc[:, :, pl.ds(index, 1), :] = (out_row[:, cut] * used).reshape(half, 2, 1, BS)
            acc[:, :, pl.ds(blocks + index, 1), :] = (in_row[:, cut] * used).reshape(half, 2, 1, BS)
    even_rows, odd_rows = acc[:, 0], acc[:, 1]
    away[...] = jnp.where(odd == 1, even_rows, odd_rows).astype(BF16)
    home[...] = jnp.where(odd == 1, odd_rows, even_rows)
    hidden = jnp.concatenate([dropped_full, grad_full], axis=0).astype(BF16)
    for mask, message in enumerate(rows):
        message[:, :BS] = hidden
        message[:, BS:] = picks[:, mask * slots * BS : (mask + 1) * slots * BS]


def all_rows(messages, half, place):
    return jnp.concatenate([block_of(message, half, place) for message in messages], axis=0)


def grad_kernel(slots, *refs):
    *messages, grad_in, grad_out, order = refs
    order[...] = jnp.zeros_like(order)
    dropped, grad_pre = all_rows(messages, 0, 0), all_rows(messages, 1, 0)
    for j in range(slots):
        grad_in[0, j] = dot(all_rows(messages, 0, 1 + j), grad_pre, ((0,), (0,)))
        grad_out[0, j] = dot(dropped, all_rows(messages, 1, 1 + j), ((0,), (0,)))


def last_kernel(blocks, kept, got, order, outputs, input_grad):
    for row in range(kept.shape[0]):
        total = kept[row] + got[row].astype(F32)
        for result, start in ((outputs, 0), (input_grad, blocks)):
            line = [total[start + i : start + i + 1] for i in range(blocks)]
            result[row : row + 1] = jnp.concatenate(line, axis=1).astype(BF16)


def call(kernel, n_vmem, out_shape, flops, nbytes, scalars=0, scratch=()):
    vmem = pl.BlockSpec(memory_space=pltpu.VMEM)
    head = [pl.BlockSpec(memory_space=pltpu.SMEM)] * scalars
    return pl.pallas_call(
        kernel,
        out_shape=out_shape,
        in_specs=head + [vmem] * n_vmem,
        out_specs=jax.tree.map(lambda _: vmem, out_shape),
        scratch_shapes=list(scratch),
        compiler_params=pltpu.CompilerParams(vmem_limit_bytes=VMEM_LIMIT),
        cost_estimate=pl.CostEstimate(flops=flops, bytes_accessed=nbytes, transcendentals=0),
    )


def flip(value, axis, size, mask):
    return lax.ppermute(value, axis, [(i, i ^ mask) for i in range(size)]) if mask else value


def gather(values, held, n_dp, orders):
    pieces = [{0: value} for value in values]
    for step, bits in enumerate(zip(*orders)):
        pieces = [
            {**parts, **{mask | bit: flip(part, "dp", n_dp, bit) for mask, part in parts.items()}}
            for parts, bit in zip(pieces, bits)
        ]
        if step == 0:
            for parts, own in zip(pieces, held):
                parts[0] = own
    for parts, value in zip(pieces, values):
        parts[0] = value
    return pieces


def exchange(messages, n_dp, bits):
    for bit in bits:
        size = messages[0].shape[1]
        leaving = jnp.concatenate([message for mask, message in enumerate(messages) if mask & bit], axis=1)
        arrived = flip(leaving, "dp", n_dp, bit)
        place = 0
        for mask in range(len(messages)):
            if mask & bit:
                messages[mask] = arrived[:, place * size : (place + 1) * size]
                place += 1
    return messages


def body(n_dp, n_mp, inputs, cotangent, w_in, w_out, block_index, block_count, drop_seeds):
    local, width = inputs.shape
    blocks = width // BS
    slots = w_in.shape[1]
    shape = jax.ShapeDtypeStruct
    piece_flops = 2 * local * slots * BS * BS
    piece_bytes = slots * BS * BS * 2

    bits = [1 << i for i in range(n_dp.bit_length() - 1)]
    *held, inputs, cotangent, block_index, block_count, seeds = lax.optimization_barrier(
        (w_in, w_out, inputs, cotangent, block_index, block_count, flip(drop_seeds, "mp", n_mp, 1))
    )
    firsts, seconds = gather([w_in, w_out], held, n_dp, [bits, bits[::-1]])

    rank = lax.axis_index("mp")
    keep = keep_factor(seeds, rank * BS)
    steps = [([0, bits[0]], [0, bits[-1]])]
    late = [n_dp - 1]
    steps.append([[mask for mask in range(n_dp - 1) if mask not in done] for done in steps[0]])
    weights = [[firsts[m] for m in masks_in] + [seconds[m] for m in masks_out] for masks_in, masks_out in steps[:1]]
    weights.append([seconds[m] for m in steps[1][1]] + [firsts[m] for m in steps[1][0]])
    picks, table, sums = call(
        functools.partial(select_kernel, slots, *steps[0]),
        1 + len(weights[0]),
        [
            shape((2 * local, n_dp * slots * BS), BF16),
            shape((8, BS), jnp.int32),
            shape((2 * local, BS), F32),
        ],
        0,
        0,
        scalars=1,
    )(jnp.concatenate([block_index[0], block_count]), jnp.concatenate([inputs, cotangent]), *weights[0])
    sums = call(
        functools.partial(partial_kernel, slots, *steps[1]),
        2 + len(weights[1]),
        shape((2 * local, BS), F32),
        0,
        0,
    )(picks, *weights[1], sums)

    half = local // 2
    masks_in, masks_out = sorted(firsts), sorted(seconds)
    away, home, *rows = call(
        functools.partial(hidden_kernel, slots, blocks, masks_in, masks_out, late),
        4 + 2 * n_dp,
        [shape((half, 2 * blocks, BS), BF16), shape((half, 2 * blocks, BS), F32)]
        + [shape((2 * local, (1 + slots) * BS), BF16)] * n_dp,
        (2 * n_dp + 2) * piece_flops,
        2 * n_dp * piece_bytes,
        scratch=[pltpu.VMEM((half, 2, 2 * blocks, BS), F32)],
    )(picks, table, keep, sums, *[firsts[m] for m in masks_in], *[seconds[m] for m in masks_out])

    total = home + flip(away, "mp", n_mp, 1).astype(F32)
    messages = exchange(rows, n_dp, bits)
    bit = n_mp // 2
    while bit > 1:
        mine_bit = (rank // bit) % 2
        cut = total.shape[0] // 2
        away = lax.dynamic_slice_in_dim(total, (1 - mine_bit) * cut, cut, 0)
        home = lax.dynamic_slice_in_dim(total, mine_bit * cut, cut, 0)
        got = flip(away.astype(BF16), "mp", n_mp, bit)
        total = home + got.astype(F32)
        bit //= 2

    grad_shape = shape((1, slots, BS, BS), F32)
    grad_in, grad_out, order = call(
        functools.partial(grad_kernel, slots),
        n_dp,
        [grad_shape, grad_shape, shape((8, BS), F32)],
        2 * n_dp * piece_flops,
        4 * piece_bytes,
    )(*messages)
    done = home.shape[0]
    outputs, input_grad = call(
        functools.partial(last_kernel, blocks),
        3,
        [shape((done, width), BF16), shape((done, width), BF16)],
        done * 2 * width,
        done * 2 * width * 8,
    )(home, got, order)
    return (outputs, input_grad, grad_in, grad_out)


def solution(mesh):
    placed = (
        P("dp", None),
        P("dp", None),
        P("mp", "dp", None, None),
        P("mp", "dp", None, None),
        P("mp", None),
        P("mp"),
        P("dp"),
    )
    return jax.shard_map(
        functools.partial(body, mesh.shape["dp"], mesh.shape["mp"]),
        mesh=mesh,
        in_specs=placed,
        out_specs=(
            P(("dp", "mp"), None),
            P(("dp", "mp"), None),
            P("mp", "dp", None, None),
            P("mp", "dp", None, None),
        ),
        check_vma=False,
    )
```

```python
import functools
import math

import jax
import jax.numpy as jnp
from jax import lax
from jax.experimental import pallas as pl
from jax.experimental.pallas import tpu as pltpu
from jax.sharding import PartitionSpec as P

BS = 128
F32 = jnp.float32
BF16 = jnp.bfloat16
VMEM_LIMIT = 48 * 2**20


def scramble(value):
    value = value ^ lax.shift_right_logical(value, jnp.int32(16))
    value = value * jnp.int32(73244475)
    value = value ^ lax.shift_right_logical(value, jnp.int32(16))
    value = value * jnp.int32(73244475)
    value = value ^ lax.shift_right_logical(value, jnp.int32(16))
    return value


def keep_factor(seeds, first_unit):
    units = first_unit + jnp.arange(BS, dtype=jnp.int32)
    mixed = scramble(seeds[:, None] + units[None, :] * jnp.int32(668265261))
    kept = mixed & jnp.int32(7) != jnp.int32(0)
    return kept.astype(F32) * jnp.float32(8.0 / 7.0)


def gelu_parts(pre_act):
    coeff = math.sqrt(2.0 / math.pi)
    inner = coeff * (pre_act + 0.044715 * pre_act**3)
    tanh_val = jnp.tanh(inner)
    activation = 0.5 * pre_act * (1.0 + tanh_val)
    slope = 0.5 * (1.0 + tanh_val) + 0.5 * pre_act * (1.0 - tanh_val * tanh_val) * coeff * (
        1.0 + 3.0 * 0.044715 * pre_act * pre_act
    )
    return (activation, slope)


def dot(left, right, dims):
    return lax.dot_general(left, right, (dims, ((), ())), preferred_element_type=F32)


def slot(listed, count, first, at):
    number = first ^ at
    return listed[number], (number < listed[count]).astype(F32)


def block_of(picks, half, place):
    local = picks.shape[0] // 2
    rows = picks[:, place * BS : (place + 1) * BS].astype(F32)
    return rows[half * local : (half + 1) * local].astype(BF16)


def side_by_side(weights, slots):
    return jnp.concatenate([weights[0, j] for j in range(slots)], axis=1)


def stacked(weights, slots):
    return weights[0].reshape(slots * BS, BS)


def add_slots(slots, picks, pre, grad, masks_in, masks_out, firsts, seconds):
    local = picks.shape[0] // 2
    span = slots * BS
    for mask, first in zip(masks_in, firsts):
        rows = picks[:, mask * span : (mask + 1) * span].astype(F32)[:local].astype(BF16)
        pre += dot(rows, stacked(first, slots), ((1,), (0,)))
    for mask, second in zip(masks_out, seconds):
        rows = picks[:, mask * span : (mask + 1) * span].astype(F32)[local:].astype(BF16)
        grad += dot(rows, side_by_side(second, slots), ((1,), (1,)))
    return pre, grad


def select_kernel(slots, masks_in, masks_out, listed, tokens, *refs):
    *weights, picks, table, sums = refs
    first = lax.axis_index("dp") * slots
    local = sums.shape[0] // 2
    row = lax.broadcasted_iota(jnp.int32, table.shape, 0)
    lane = lax.broadcasted_iota(jnp.int32, table.shape, 1)
    entries = jnp.zeros(table.shape, jnp.int32)
    count = picks.shape[1] // BS
    for place in range(count):
        index, used = slot(listed, count, first, place)
        at = pl.ds(pl.multiple_of(index * BS, BS), BS)
        picks[:, place * BS : (place + 1) * BS] = (tokens[:, at].astype(F32) * used).astype(BF16)
        entry = jnp.where(row == 0, index, used.astype(jnp.int32))
        entries = jnp.where(lane == place, entry, entries)
    table[...] = entries
    zero = jnp.zeros((local, BS), F32)
    firsts, seconds = weights[: len(masks_in)], weights[len(masks_in) :]
    pre, grad = add_slots(slots, picks, zero, zero, masks_in, masks_out, firsts, seconds)
    sums[:local] = pre
    sums[local:] = grad


def partial_kernel(slots, masks_in, masks_out, picks, *refs):
    *weights, sums, out = refs
    local = picks.shape[0] // 2
    seconds, firsts = weights[: len(masks_out)], weights[len(masks_out) :]
    pre, grad = add_slots(slots, picks, sums[:local], sums[local:], masks_in, masks_out, firsts, seconds)
    out[:local] = pre
    out[local:] = grad


def hidden_kernel(slots, blocks, masks_in, masks_out, late, picks, table, keep, sums, *refs):
    count = len(masks_in)
    firsts = dict(zip(masks_in, refs[:count]))
    seconds = dict(zip(masks_out, refs[count : 2 * count]))
    away, home, *rows = refs[2 * count : -1]
    acc = refs[-1]
    local = keep.shape[0]
    half = local // 2
    odd = lax.axis_index("mp") % 2
    acc[...] = jnp.zeros_like(acc)
    entries = table[...]
    pre, grad = add_slots(
        slots, picks, sums[:local], sums[local:], late, late, [firsts[m] for m in late], [seconds[m] for m in late]
    )
    activation, slope = gelu_parts(pre)
    dropped_full = activation * keep[...]
    grad_full = grad * keep[...] * slope
    dropped, grad_pre = dropped_full.astype(BF16), grad_full.astype(BF16)
    for mask in range(count):
        out_row = dot(dropped, side_by_side(seconds[mask], slots), ((1,), (0,)))
        in_row = dot(grad_pre, stacked(firsts[mask], slots), ((1,), (1,)))
        for j in range(slots):
            at = mask * slots + j
            index, used = entries[0, at], entries[1, at].astype(F32)
            cut = slice(j * BS, (j + 1) * BS)
            acc[:, :, pl.ds(index, 1), :] = (out_row[:, cut] * used).reshape(half, 2, 1, BS)
            acc[:, :, pl.ds(blocks + index, 1), :] = (in_row[:, cut] * used).reshape(half, 2, 1, BS)
    even_rows, odd_rows = acc[:, 0], acc[:, 1]
    away[...] = jnp.where(odd == 1, even_rows, odd_rows).astype(BF16)
    home[...] = jnp.where(odd == 1, odd_rows, even_rows)
    hidden = jnp.concatenate([dropped_full, grad_full], axis=0).astype(BF16)
    for mask, message in enumerate(rows):
        message[:, :BS] = hidden
        message[:, BS:] = picks[:, mask * slots * BS : (mask + 1) * slots * BS]


def all_rows(messages, half, place):
    return jnp.concatenate([block_of(message, half, place) for message in messages], axis=0)


def grad_kernel(slots, *refs):
    *messages, grad_in, grad_out, order = refs
    order[...] = jnp.zeros_like(order)
    dropped, grad_pre = all_rows(messages, 0, 0), all_rows(messages, 1, 0)
    for j in range(slots):
        grad_in[0, j] = dot(all_rows(messages, 0, 1 + j), grad_pre, ((0,), (0,)))
        grad_out[0, j] = dot(dropped, all_rows(messages, 1, 1 + j), ((0,), (0,)))


def last_kernel(blocks, kept, got, order, outputs, input_grad):
    for row in range(kept.shape[0]):
        total = kept[row] + got[row].astype(F32)
        for result, start in ((outputs, 0), (input_grad, blocks)):
            line = [total[start + i : start + i + 1] for i in range(blocks)]
            result[row : row + 1] = jnp.concatenate(line, axis=1).astype(BF16)


def call(kernel, n_vmem, out_shape, flops, nbytes, scalars=0, scratch=()):
    vmem = pl.BlockSpec(memory_space=pltpu.VMEM)
    head = [pl.BlockSpec(memory_space=pltpu.SMEM)] * scalars
    return pl.pallas_call(
        kernel,
        out_shape=out_shape,
        in_specs=head + [vmem] * n_vmem,
        out_specs=jax.tree.map(lambda _: vmem, out_shape),
        scratch_shapes=list(scratch),
        compiler_params=pltpu.CompilerParams(vmem_limit_bytes=VMEM_LIMIT),
        cost_estimate=pl.CostEstimate(flops=flops, bytes_accessed=nbytes, transcendentals=0),
    )


def flip(value, axis, size, mask):
    return lax.ppermute(value, axis, [(i, i ^ mask) for i in range(size)]) if mask else value


def gather(values, held, n_dp, orders):
    pieces = [{0: value} for value in values]
    for step, bits in enumerate(zip(*orders)):
        pieces = [
            {**parts, **{mask | bit: flip(part, "dp", n_dp, bit) for mask, part in parts.items()}}
            for parts, bit in zip(pieces, bits)
        ]
        if step == 0:
            for parts, own in zip(pieces, held):
                parts[0] = own
    for parts, value in zip(pieces, values):
        parts[0] = value
        for mask in parts:
            parts[mask] = parts[mask].reshape(value.shape)
    return pieces


def exchange(messages, n_dp, bits):
    for bit in bits:
        size = messages[0].shape[1]
        leaving = jnp.concatenate([message for mask, message in enumerate(messages) if mask & bit], axis=1)
        arrived = flip(leaving, "dp", n_dp, bit)
        place = 0
        for mask in range(len(messages)):
            if mask & bit:
                messages[mask] = arrived[:, place * size : (place + 1) * size]
                place += 1
    return messages


def body(n_dp, n_mp, inputs, cotangent, w_in, w_out, block_index, block_count, drop_seeds):
    local, width = inputs.shape
    blocks = width // BS
    slots = w_in.shape[1]
    shape = jax.ShapeDtypeStruct
    piece_flops = 2 * local * slots * BS * BS
    piece_bytes = slots * BS * BS * 2

    bits = [1 << i for i in range(n_dp.bit_length() - 1)]
    firsts, seconds = gather([w_in, w_out], [w_in[0], w_out[0]], n_dp, [bits, bits[::-1]])

    rank = lax.axis_index("mp")
    keep = keep_factor(drop_seeds, rank * BS)
    steps = [([0, bits[0]], [0, bits[-1]])]
    late = [n_dp - 1]
    steps.append([[mask for mask in range(n_dp - 1) if mask not in done] for done in steps[0]])
    weights = [[firsts[m] for m in masks_in] + [seconds[m] for m in masks_out] for masks_in, masks_out in steps[:1]]
    weights.append([seconds[m] for m in steps[1][1]] + [firsts[m] for m in steps[1][0]])
    picks, table, sums = call(
        functools.partial(select_kernel, slots, *steps[0]),
        1 + len(weights[0]),
        [
            shape((2 * local, n_dp * slots * BS), BF16),
            shape((8, BS), jnp.int32),
            shape((2 * local, BS), F32),
        ],
        0,
        0,
        scalars=1,
    )(jnp.concatenate([block_index[0], block_count]), jnp.concatenate([inputs, cotangent]), *weights[0])
    sums = call(
        functools.partial(partial_kernel, slots, *steps[1]),
        2 + len(weights[1]),
        shape((2 * local, BS), F32),
        0,
        0,
    )(picks, *weights[1], sums)

    half = local // 2
    masks_in, masks_out = sorted(firsts), sorted(seconds)
    away, home, *rows = call(
        functools.partial(hidden_kernel, slots, blocks, masks_in, masks_out, late),
        4 + 2 * n_dp,
        [shape((half, 2 * blocks, BS), BF16), shape((half, 2 * blocks, BS), F32)]
        + [shape((2 * local, (1 + slots) * BS), BF16)] * n_dp,
        (2 * n_dp + 2) * piece_flops,
        2 * n_dp * piece_bytes,
        scratch=[pltpu.VMEM((half, 2, 2 * blocks, BS), F32)],
    )(picks, table, keep, sums, *[firsts[m] for m in masks_in], *[seconds[m] for m in masks_out])

    total = home + flip(away, "mp", n_mp, 1).astype(F32)
    messages = exchange(rows, n_dp, bits)
    bit = n_mp // 2
    while bit > 1:
        mine_bit = (rank // bit) % 2
        cut = total.shape[0] // 2
        away = lax.dynamic_slice_in_dim(total, (1 - mine_bit) * cut, cut, 0)
        home = lax.dynamic_slice_in_dim(total, mine_bit * cut, cut, 0)
        got = flip(away.astype(BF16), "mp", n_mp, bit)
        total = home + got.astype(F32)
        bit //= 2

    grad_shape = shape((1, slots, BS, BS), F32)
    grad_in, grad_out, order = call(
        functools.partial(grad_kernel, slots),
        n_dp,
        [grad_shape, grad_shape, shape((8, BS), F32)],
        2 * n_dp * piece_flops,
        4 * piece_bytes,
    )(*messages)
    done = home.shape[0]
    outputs, input_grad = call(
        functools.partial(last_kernel, blocks),
        3,
        [shape((done, width), BF16), shape((done, width), BF16)],
        done * 2 * width,
        done * 2 * width * 8,
    )(home, got, order)
    return (outputs, input_grad, grad_in, grad_out)


def solution(mesh):
    placed = (
        P("dp", None),
        P("dp", None),
        P("mp", "dp", None, None),
        P("mp", "dp", None, None),
        P("mp", None),
        P("mp"),
        P("dp"),
    )
    return jax.shard_map(
        functools.partial(body, mesh.shape["dp"], mesh.shape["mp"]),
        mesh=mesh,
        in_specs=placed,
        out_specs=(
            P(("dp", "mp"), None),
            P(("dp", "mp"), None),
            P("mp", "dp", None, None),
            P("mp", "dp", None, None),
        ),
        check_vma=False,
    )
```

```python
import functools
import math

import jax
import jax.numpy as jnp
from jax import lax
from jax.experimental import pallas as pl
from jax.experimental.pallas import tpu as pltpu
from jax.sharding import PartitionSpec as P

BS = 128
F32 = jnp.float32
BF16 = jnp.bfloat16
VMEM_LIMIT = 48 * 2**20


def scramble(value):
    value = value ^ lax.shift_right_logical(value, jnp.int32(16))
    value = value * jnp.int32(73244475)
    value = value ^ lax.shift_right_logical(value, jnp.int32(16))
    value = value * jnp.int32(73244475)
    value = value ^ lax.shift_right_logical(value, jnp.int32(16))
    return value


def keep_factor(seeds, first_unit):
    units = first_unit + jnp.arange(BS, dtype=jnp.int32)
    mixed = scramble(seeds[:, None] + units[None, :] * jnp.int32(668265261))
    kept = mixed & jnp.int32(7) != jnp.int32(0)
    return kept.astype(F32) * jnp.float32(8.0 / 7.0)


def gelu_parts(pre_act):
    coeff = math.sqrt(2.0 / math.pi)
    inner = coeff * (pre_act + 0.044715 * pre_act**3)
    tanh_val = jnp.tanh(inner)
    activation = 0.5 * pre_act * (1.0 + tanh_val)
    slope = 0.5 * (1.0 + tanh_val) + 0.5 * pre_act * (1.0 - tanh_val * tanh_val) * coeff * (
        1.0 + 3.0 * 0.044715 * pre_act * pre_act
    )
    return (activation, slope)


def dot(left, right, dims):
    return lax.dot_general(left, right, (dims, ((), ())), preferred_element_type=F32)


def slot(listed, count, first, at):
    number = first ^ at
    return listed[number], (number < listed[count]).astype(F32)


def block_of(picks, half, place):
    local = picks.shape[0] // 2
    rows = picks[:, place * BS : (place + 1) * BS].astype(F32)
    return rows[half * local : (half + 1) * local].astype(BF16)


def side_by_side(weights, slots):
    return jnp.concatenate([weights[0, j] for j in range(slots)], axis=1)


def stacked(weights, slots):
    return weights[0].reshape(slots * BS, BS)


def add_slots(slots, picks, pre, grad, masks_in, masks_out, firsts, seconds):
    local = picks.shape[0] // 2
    span = slots * BS
    for mask, first in zip(masks_in, firsts):
        rows = picks[:, mask * span : (mask + 1) * span].astype(F32)[:local].astype(BF16)
        pre += dot(rows, stacked(first, slots), ((1,), (0,)))
    for mask, second in zip(masks_out, seconds):
        rows = picks[:, mask * span : (mask + 1) * span].astype(F32)[local:].astype(BF16)
        grad += dot(rows, side_by_side(second, slots), ((1,), (1,)))
    return pre, grad


def select_kernel(slots, masks_in, masks_out, listed, tokens, *refs):
    *weights, picks, table, sums = refs
    first = lax.axis_index("dp") * slots
    local = sums.shape[0] // 2
    row = lax.broadcasted_iota(jnp.int32, table.shape, 0)
    lane = lax.broadcasted_iota(jnp.int32, table.shape, 1)
    entries = jnp.zeros(table.shape, jnp.int32)
    count = picks.shape[1] // BS
    for place in range(count):
        index, used = slot(listed, count, first, place)
        at = pl.ds(pl.multiple_of(index * BS, BS), BS)
        picks[:, place * BS : (place + 1) * BS] = (tokens[:, at].astype(F32) * used).astype(BF16)
        entry = jnp.where(row == 0, index, used.astype(jnp.int32))
        entries = jnp.where(lane == place, entry, entries)
    table[...] = entries
    zero = jnp.zeros((local, BS), F32)
    firsts, seconds = weights[: len(masks_in)], weights[len(masks_in) :]
    pre, grad = add_slots(slots, picks, zero, zero, masks_in, masks_out, firsts, seconds)
    sums[:local] = pre
    sums[local:] = grad


def partial_kernel(slots, masks_in, masks_out, picks, *refs):
    *weights, sums, out = refs
    local = picks.shape[0] // 2
    seconds, firsts = weights[: len(masks_out)], weights[len(masks_out) :]
    pre, grad = add_slots(slots, picks, sums[:local], sums[local:], masks_in, masks_out, firsts, seconds)
    out[:local] = pre
    out[local:] = grad


def bit_parity(number, size):
    return functools.reduce(lambda found, i: found ^ number >> i & 1, range(1, size.bit_length()), number & 1)


def hidden_kernel(slots, blocks, masks_in, masks_out, late, picks, table, keep, sums, *refs):
    count = len(masks_in)
    firsts = dict(zip(masks_in, refs[:count]))
    seconds = dict(zip(masks_out, refs[count : 2 * count]))
    away, home, *rows = refs[2 * count : -1]
    acc = refs[-1]
    local = keep.shape[0]
    half = local // 2
    acc[...] = jnp.zeros_like(acc)
    entries = table[...]
    pre, grad = add_slots(
        slots, picks, sums[:local], sums[local:], late, late, [firsts[m] for m in late], [seconds[m] for m in late]
    )
    activation, slope = gelu_parts(pre)
    dropped_full = activation * keep[...]
    grad_full = grad * keep[...] * slope
    dropped, grad_pre = dropped_full.astype(BF16), grad_full.astype(BF16)
    for mask in range(count):
        out_row = dot(dropped, side_by_side(seconds[mask], slots), ((1,), (0,)))
        in_row = dot(grad_pre, stacked(firsts[mask], slots), ((1,), (1,)))
        for j in range(slots):
            at = mask * slots + j
            index, used = entries[0, at], entries[1, at].astype(F32)
            cut = slice(j * BS, (j + 1) * BS)
            acc[:, :, pl.ds(index, 1), :] = (out_row[:, cut] * used).reshape(half, 2, 1, BS)
            acc[:, :, pl.ds(blocks + index, 1), :] = (in_row[:, cut] * used).reshape(half, 2, 1, BS)
    odd = bit_parity(lax.axis_index("mp"), 2 * half)
    for i in range(half):
        even_row, odd_row = acc[i, bit_parity(i, half)], acc[i, 1 - bit_parity(i, half)]
        away[i] = jnp.where(odd == 1, even_row, odd_row).astype(BF16)
        home[i] = jnp.where(odd == 1, odd_row, even_row)
    hidden = jnp.concatenate([dropped_full, grad_full], axis=0).astype(BF16)
    for mask, message in enumerate(rows):
        message[:, :BS] = hidden
        message[:, BS:] = picks[:, mask * slots * BS : (mask + 1) * slots * BS]


def all_rows(messages, half, place):
    return jnp.concatenate([block_of(message, half, place) for message in messages], axis=0)


def grad_kernel(slots, *refs):
    *messages, grad_in, grad_out, order = refs
    order[...] = jnp.zeros_like(order)
    dropped, grad_pre = all_rows(messages, 0, 0), all_rows(messages, 1, 0)
    for j in range(slots):
        grad_in[0, j] = dot(all_rows(messages, 0, 1 + j), grad_pre, ((0,), (0,)))
        grad_out[0, j] = dot(dropped, all_rows(messages, 1, 1 + j), ((0,), (0,)))


def last_kernel(blocks, kept, got, order, outputs, input_grad):
    for row in range(kept.shape[0]):
        total = kept[row] + got[row].astype(F32)
        for result, start in ((outputs, 0), (input_grad, blocks)):
            line = [total[start + i : start + i + 1] for i in range(blocks)]
            result[row : row + 1] = jnp.concatenate(line, axis=1).astype(BF16)


def call(kernel, n_vmem, out_shape, flops, nbytes, scalars=0, scratch=()):
    vmem = pl.BlockSpec(memory_space=pltpu.VMEM)
    head = [pl.BlockSpec(memory_space=pltpu.SMEM)] * scalars
    return pl.pallas_call(
        kernel,
        out_shape=out_shape,
        in_specs=head + [vmem] * n_vmem,
        out_specs=jax.tree.map(lambda _: vmem, out_shape),
        scratch_shapes=list(scratch),
        compiler_params=pltpu.CompilerParams(vmem_limit_bytes=VMEM_LIMIT),
        cost_estimate=pl.CostEstimate(flops=flops, bytes_accessed=nbytes, transcendentals=0),
    )


def flip(value, axis, size, mask):
    return lax.ppermute(value, axis, [(i, i ^ mask) for i in range(size)]) if mask else value


def gather(values, held, n_dp, orders):
    pieces = [{0: value} for value in values]
    for step, bits in enumerate(zip(*orders)):
        pieces = [
            {**parts, **{mask | bit: flip(part, "dp", n_dp, bit) for mask, part in parts.items()}}
            for parts, bit in zip(pieces, bits)
        ]
        if step == 0:
            for parts, own in zip(pieces, held):
                parts[0] = own
    for parts, value in zip(pieces, values):
        parts[0] = value
        for mask in parts:
            parts[mask] = parts[mask].reshape(value.shape)
    return pieces


def exchange(messages, n_dp, bits):
    for bit in bits:
        size = messages[0].shape[1]
        leaving = jnp.concatenate([message for mask, message in enumerate(messages) if mask & bit], axis=1)
        arrived = flip(leaving, "dp", n_dp, bit)
        place = 0
        for mask in range(len(messages)):
            if mask & bit:
                messages[mask] = arrived[:, place * size : (place + 1) * size]
                place += 1
    return messages


def body(n_dp, n_mp, inputs, cotangent, w_in, w_out, block_index, block_count, drop_seeds):
    local, width = inputs.shape
    blocks = width // BS
    slots = w_in.shape[1]
    shape = jax.ShapeDtypeStruct
    piece_flops = 2 * local * slots * BS * BS
    piece_bytes = slots * BS * BS * 2

    bits = [1 << i for i in range(n_dp.bit_length() - 1)]
    firsts, seconds = gather([w_in, w_out], [w_in[0], w_out[0]], n_dp, [bits, bits[::-1]])

    rank = lax.axis_index("mp")
    keep = keep_factor(drop_seeds, rank * BS)
    steps = [([0, bits[0]], [0, bits[-1]])]
    late = [n_dp - 1]
    steps.append([[mask for mask in range(n_dp - 1) if mask not in done] for done in steps[0]])
    weights = [[firsts[m] for m in masks_in] + [seconds[m] for m in masks_out] for masks_in, masks_out in steps[:1]]
    weights.append([seconds[m] for m in steps[1][1]] + [firsts[m] for m in steps[1][0]])
    picks, table, sums = call(
        functools.partial(select_kernel, slots, *steps[0]),
        1 + len(weights[0]),
        [
            shape((2 * local, n_dp * slots * BS), BF16),
            shape((8, BS), jnp.int32),
            shape((2 * local, BS), F32),
        ],
        0,
        0,
        scalars=1,
    )(jnp.concatenate([block_index[0], block_count]), jnp.concatenate([inputs, cotangent]), *weights[0])
    sums = call(
        functools.partial(partial_kernel, slots, *steps[1]),
        2 + len(weights[1]),
        shape((2 * local, BS), F32),
        0,
        0,
    )(picks, *weights[1], sums)

    half = local // 2
    masks_in, masks_out = sorted(firsts), sorted(seconds)
    away, home, *rows = call(
        functools.partial(hidden_kernel, slots, blocks, masks_in, masks_out, late),
        4 + 2 * n_dp,
        [shape((half, 2 * blocks, BS), BF16), shape((half, 2 * blocks, BS), F32)]
        + [shape((2 * local, (1 + slots) * BS), BF16)] * n_dp,
        (2 * n_dp + 2) * piece_flops,
        2 * n_dp * piece_bytes,
        scratch=[pltpu.VMEM((half, 2, 2 * blocks, BS), F32)],
    )(picks, table, keep, sums, *[firsts[m] for m in masks_in], *[seconds[m] for m in masks_out])

    total = home + flip(away, "mp", n_mp, 1).astype(F32)
    messages = exchange(rows, n_dp, bits)
    bit = n_mp // 2
    while bit > 1:
        mine_bit = (rank // bit) % 2
        cut = total.shape[0] // 2
        away = lax.dynamic_slice_in_dim(total, (1 - mine_bit) * cut, cut, 0)
        home = lax.dynamic_slice_in_dim(total, mine_bit * cut, cut, 0)
        got = flip(away.astype(BF16), "mp", n_mp, bit | 1)
        total = home + got.astype(F32)
        bit //= 2

    grad_shape = shape((1, slots, BS, BS), F32)
    grad_in, grad_out, order = call(
        functools.partial(grad_kernel, slots),
        n_dp,
        [grad_shape, grad_shape, shape((8, BS), F32)],
        2 * n_dp * piece_flops,
        4 * piece_bytes,
    )(*messages)
    done = home.shape[0]
    outputs, input_grad = call(
        functools.partial(last_kernel, blocks),
        3,
        [shape((done, width), BF16), shape((done, width), BF16)],
        done * 2 * width,
        done * 2 * width * 8,
    )(home, got, order)
    return (outputs, input_grad, grad_in, grad_out)


def solution(mesh):
    placed = (
        P("dp", None),
        P("dp", None),
        P("mp", "dp", None, None),
        P("mp", "dp", None, None),
        P("mp", None),
        P("mp"),
        P("dp"),
    )
    return jax.shard_map(
        functools.partial(body, mesh.shape["dp"], mesh.shape["mp"]),
        mesh=mesh,
        in_specs=placed,
        out_specs=(
            P(("dp", "mp"), None),
            P(("dp", "mp"), None),
            P("mp", "dp", None, None),
            P("mp", "dp", None, None),
        ),
        check_vma=False,
    )
```

```python
import functools
import math

import jax
import jax.numpy as jnp
from jax import lax
from jax.experimental import pallas as pl
from jax.experimental.pallas import tpu as pltpu
from jax.sharding import PartitionSpec as P

BS = 128
F32 = jnp.float32
BF16 = jnp.bfloat16
VMEM_LIMIT = 48 * 2**20


def scramble(value):
    value = value ^ lax.shift_right_logical(value, jnp.int32(16))
    value = value * jnp.int32(73244475)
    value = value ^ lax.shift_right_logical(value, jnp.int32(16))
    value = value * jnp.int32(73244475)
    value = value ^ lax.shift_right_logical(value, jnp.int32(16))
    return value


def keep_factor(seeds, first_unit):
    units = first_unit + jnp.arange(BS, dtype=jnp.int32)
    mixed = scramble(seeds[:, None] + units[None, :] * jnp.int32(668265261))
    kept = mixed & jnp.int32(7) != jnp.int32(0)
    return kept.astype(F32) * jnp.float32(8.0 / 7.0)


def gelu_parts(pre_act):
    coeff = math.sqrt(2.0 / math.pi)
    inner = coeff * (pre_act + 0.044715 * pre_act**3)
    tanh_val = jnp.tanh(inner)
    activation = 0.5 * pre_act * (1.0 + tanh_val)
    slope = 0.5 * (1.0 + tanh_val) + 0.5 * pre_act * (1.0 - tanh_val * tanh_val) * coeff * (
        1.0 + 3.0 * 0.044715 * pre_act * pre_act
    )
    return (activation, slope)


def dot(left, right, dims):
    return lax.dot_general(left, right, (dims, ((), ())), preferred_element_type=F32)


def slot(listed, count, first, at):
    number = first ^ at
    return listed[number], (number < listed[count]).astype(F32)


def block_of(picks, half, place):
    local = picks.shape[0] // 2
    rows = picks[:, place * BS : (place + 1) * BS].astype(F32)
    return rows[half * local : (half + 1) * local].astype(BF16)


def side_by_side(weights, slots):
    return jnp.concatenate([weights[0, j] for j in range(slots)], axis=1)


def stacked(weights, slots):
    return weights[0].reshape(slots * BS, BS)


def add_slots(slots, picks, pre, grad, masks_in, masks_out, firsts, seconds):
    local = picks.shape[0] // 2
    span = slots * BS
    for mask, first in zip(masks_in, firsts):
        rows = picks[:, mask * span : (mask + 1) * span].astype(F32)[:local].astype(BF16)
        pre += dot(rows, stacked(first, slots), ((1,), (0,)))
    for mask, second in zip(masks_out, seconds):
        rows = picks[:, mask * span : (mask + 1) * span].astype(F32)[local:].astype(BF16)
        grad += dot(rows, side_by_side(second, slots), ((1,), (1,)))
    return pre, grad


def select_kernel(slots, masks_in, masks_out, listed, tokens, *refs):
    *weights, picks, table, sums = refs
    first = lax.axis_index("dp") * slots
    local = sums.shape[0] // 2
    row = lax.broadcasted_iota(jnp.int32, table.shape, 0)
    lane = lax.broadcasted_iota(jnp.int32, table.shape, 1)
    entries = jnp.zeros(table.shape, jnp.int32)
    odd = lax.axis_index("mp") % 2
    count = picks.shape[1] // BS
    for place in range(count):
        mask = place // slots
        turned = (mirrored(mask, count // slots) - mask) * slots
        index, used = slot(listed, count, first, place + odd * turned)
        at = pl.ds(pl.multiple_of(index * BS, BS), BS)
        picks[:, place * BS : (place + 1) * BS] = (tokens[:, at].astype(F32) * used).astype(BF16)
        entry = jnp.where(row == 0, index, used.astype(jnp.int32))
        entries = jnp.where(lane == place, entry, entries)
    table[...] = entries
    zero = jnp.zeros((local, BS), F32)
    firsts, seconds = weights[: len(masks_in)], weights[len(masks_in) :]
    pre, grad = add_slots(slots, picks, zero, zero, masks_in, masks_out, firsts, seconds)
    sums[:local] = pre
    sums[local:] = grad


def partial_kernel(slots, masks_in, masks_out, picks, *refs):
    *weights, sums, out = refs
    local = picks.shape[0] // 2
    seconds, firsts = weights[: len(masks_out)], weights[len(masks_out) :]
    pre, grad = add_slots(slots, picks, sums[:local], sums[local:], masks_in, masks_out, firsts, seconds)
    out[:local] = pre
    out[local:] = grad


def bit_parity(number, size):
    return functools.reduce(lambda found, i: found ^ number >> i & 1, range(1, size.bit_length()), number & 1)


def hidden_kernel(slots, blocks, masks_in, masks_out, late, picks, table, keep, sums, *refs):
    count = len(masks_in)
    firsts = dict(zip(masks_in, refs[:count]))
    seconds = dict(zip(masks_out, refs[count : 2 * count]))
    away, home, *rows = refs[2 * count : -1]
    acc = refs[-1]
    local = keep.shape[0]
    half = local // 2
    acc[...] = jnp.zeros_like(acc)
    entries = table[...]
    pre, grad = add_slots(
        slots, picks, sums[:local], sums[local:], late, late, [firsts[m] for m in late], [seconds[m] for m in late]
    )
    activation, slope = gelu_parts(pre)
    dropped_full = activation * keep[...]
    grad_full = grad * keep[...] * slope
    dropped, grad_pre = dropped_full.astype(BF16), grad_full.astype(BF16)
    for mask in range(count):
        out_row = dot(dropped, side_by_side(seconds[mask], slots), ((1,), (0,)))
        in_row = dot(grad_pre, stacked(firsts[mask], slots), ((1,), (1,)))
        for j in range(slots):
            at = mask * slots + j
            index, used = entries[0, at], entries[1, at].astype(F32)
            cut = slice(j * BS, (j + 1) * BS)
            acc[:, :, pl.ds(index, 1), :] = (out_row[:, cut] * used).reshape(half, 2, 1, BS)
            acc[:, :, pl.ds(blocks + index, 1), :] = (in_row[:, cut] * used).reshape(half, 2, 1, BS)
    odd = bit_parity(lax.axis_index("mp"), 2 * half)
    for i in range(half):
        even_row, odd_row = acc[i, bit_parity(i, half)], acc[i, 1 - bit_parity(i, half)]
        away[i] = jnp.where(odd == 1, even_row, odd_row).astype(BF16)
        home[i] = jnp.where(odd == 1, odd_row, even_row)
    hidden = jnp.concatenate([dropped_full, grad_full], axis=0).astype(BF16)
    for mask, message in enumerate(rows):
        message[:, :BS] = hidden
        message[:, BS:] = picks[:, mask * slots * BS : (mask + 1) * slots * BS]


def all_rows(messages, half, place):
    return jnp.concatenate([block_of(message, half, place) for message in messages], axis=0)


def grad_kernel(slots, *refs):
    *messages, grad_in, grad_out, order = refs
    order[...] = jnp.zeros_like(order)
    dropped, grad_pre = all_rows(messages, 0, 0), all_rows(messages, 1, 0)
    for j in range(slots):
        grad_in[0, j] = dot(all_rows(messages, 0, 1 + j), grad_pre, ((0,), (0,)))
        grad_out[0, j] = dot(dropped, all_rows(messages, 1, 1 + j), ((0,), (0,)))


def last_kernel(blocks, kept, got, order, outputs, input_grad):
    for row in range(kept.shape[0]):
        total = kept[row] + got[row].astype(F32)
        for result, start in ((outputs, 0), (input_grad, blocks)):
            line = [total[start + i : start + i + 1] for i in range(blocks)]
            result[row : row + 1] = jnp.concatenate(line, axis=1).astype(BF16)


def call(kernel, n_vmem, out_shape, flops, nbytes, scalars=0, scratch=()):
    vmem = pl.BlockSpec(memory_space=pltpu.VMEM)
    head = [pl.BlockSpec(memory_space=pltpu.SMEM)] * scalars
    return pl.pallas_call(
        kernel,
        out_shape=out_shape,
        in_specs=head + [vmem] * n_vmem,
        out_specs=jax.tree.map(lambda _: vmem, out_shape),
        scratch_shapes=list(scratch),
        compiler_params=pltpu.CompilerParams(vmem_limit_bytes=VMEM_LIMIT),
        cost_estimate=pl.CostEstimate(flops=flops, bytes_accessed=nbytes, transcendentals=0),
    )


def flip(value, axis, size, mask):
    return lax.ppermute(value, axis, [(i, i ^ mask) for i in range(size)]) if mask else value


def mirrored(mask, n_dp):
    width = n_dp.bit_length() - 1
    return sum(1 << (width - 1 - i) for i in range(width) if mask >> i & 1)


def cross(value, n_dp, n_mp, mask):
    pairs = []
    for i in range(n_dp):
        for j in range(n_mp):
            other = i ^ (mirrored(mask, n_dp) if j % 2 else mask)
            pairs.append((i * n_mp + j, other * n_mp + j))
    return lax.ppermute(value, ("dp", "mp"), pairs)


def gather(values, held, n_dp, n_mp, orders):
    pieces = [{0: value} for value in values]
    for step, bits in enumerate(zip(*orders)):
        pieces = [
            {**parts, **{mask | bit: cross(part, n_dp, n_mp, bit) for mask, part in parts.items()}}
            for parts, bit in zip(pieces, bits)
        ]
        if step == 0:
            for parts, own in zip(pieces, held):
                parts[0] = own
    for parts, value in zip(pieces, values):
        parts[0] = value
        for mask in parts:
            parts[mask] = parts[mask].reshape(value.shape)
    return pieces


def exchange(messages, n_dp, n_mp, bits):
    for bit in bits:
        size = messages[0].shape[1]
        leaving = jnp.concatenate([message for mask, message in enumerate(messages) if mask & bit], axis=1)
        arrived = cross(leaving, n_dp, n_mp, bit)
        place = 0
        for mask in range(len(messages)):
            if mask & bit:
                messages[mask] = arrived[:, place * size : (place + 1) * size]
                place += 1
    return messages


def body(n_dp, n_mp, inputs, cotangent, w_in, w_out, block_index, block_count, drop_seeds):
    local, width = inputs.shape
    blocks = width // BS
    slots = w_in.shape[1]
    shape = jax.ShapeDtypeStruct
    piece_flops = 2 * local * slots * BS * BS
    piece_bytes = slots * BS * BS * 2

    bits = [1 << i for i in range(n_dp.bit_length() - 1)]
    firsts, seconds = gather([w_in, w_out], [w_in[0], w_out[0]], n_dp, n_mp, [bits, bits[::-1]])

    rank = lax.axis_index("mp")
    keep = keep_factor(drop_seeds, rank * BS)
    steps = [([0, bits[0]], [0, bits[-1]])]
    late = [n_dp - 1]
    steps.append([[mask for mask in range(n_dp - 1) if mask not in done] for done in steps[0]])
    weights = [[firsts[m] for m in masks_in] + [seconds[m] for m in masks_out] for masks_in, masks_out in steps[:1]]
    weights.append([seconds[m] for m in steps[1][1]] + [firsts[m] for m in steps[1][0]])
    picks, table, sums = call(
        functools.partial(select_kernel, slots, *steps[0]),
        1 + len(weights[0]),
        [
            shape((2 * local, n_dp * slots * BS), BF16),
            shape((8, BS), jnp.int32),
            shape((2 * local, BS), F32),
        ],
        0,
        0,
        scalars=1,
    )(jnp.concatenate([block_index[0], block_count]), jnp.concatenate([inputs, cotangent]), *weights[0])
    sums = call(
        functools.partial(partial_kernel, slots, *steps[1]),
        2 + len(weights[1]),
        shape((2 * local, BS), F32),
        0,
        0,
    )(picks, *weights[1], sums)

    half = local // 2
    masks_in, masks_out = sorted(firsts), sorted(seconds)
    away, home, *rows = call(
        functools.partial(hidden_kernel, slots, blocks, masks_in, masks_out, late),
        4 + 2 * n_dp,
        [shape((half, 2 * blocks, BS), BF16), shape((half, 2 * blocks, BS), F32)]
        + [shape((2 * local, (1 + slots) * BS), BF16)] * n_dp,
        (2 * n_dp + 2) * piece_flops,
        2 * n_dp * piece_bytes,
        scratch=[pltpu.VMEM((half, 2, 2 * blocks, BS), F32)],
    )(picks, table, keep, sums, *[firsts[m] for m in masks_in], *[seconds[m] for m in masks_out])

    total = home + flip(away, "mp", n_mp, 1).astype(F32)
    messages = exchange(rows, n_dp, n_mp, bits)
    bit = n_mp // 2
    while bit > 1:
        mine_bit = (rank // bit) % 2
        cut = total.shape[0] // 2
        away = lax.dynamic_slice_in_dim(total, (1 - mine_bit) * cut, cut, 0)
        home = lax.dynamic_slice_in_dim(total, mine_bit * cut, cut, 0)
        got = flip(away.astype(BF16), "mp", n_mp, bit | 1)
        total = home + got.astype(F32)
        bit //= 2

    grad_shape = shape((1, slots, BS, BS), F32)
    grad_in, grad_out, order = call(
        functools.partial(grad_kernel, slots),
        n_dp,
        [grad_shape, grad_shape, shape((8, BS), F32)],
        2 * n_dp * piece_flops,
        4 * piece_bytes,
    )(*messages)
    done = home.shape[0]
    outputs, input_grad = call(
        functools.partial(last_kernel, blocks),
        3,
        [shape((done, width), BF16), shape((done, width), BF16)],
        done * 2 * width,
        done * 2 * width * 8,
    )(home, got, order)
    return (outputs, input_grad, grad_in, grad_out)


def solution(mesh):
    placed = (
        P("dp", None),
        P("dp", None),
        P("mp", "dp", None, None),
        P("mp", "dp", None, None),
        P("mp", None),
        P("mp"),
        P("dp"),
    )
    return jax.shard_map(
        functools.partial(body, mesh.shape["dp"], mesh.shape["mp"]),
        mesh=mesh,
        in_specs=placed,
        out_specs=(
            P(("dp", "mp"), None),
            P(("dp", "mp"), None),
            P("mp", "dp", None, None),
            P("mp", "dp", None, None),
        ),
        check_vma=False,
    )
```

```python
import functools
import math

import jax
import jax.numpy as jnp
from jax import lax
from jax.experimental import pallas as pl
from jax.experimental.pallas import tpu as pltpu
from jax.sharding import PartitionSpec as P

BS = 128
F32 = jnp.float32
BF16 = jnp.bfloat16
VMEM_LIMIT = 48 * 2**20


def scramble(value):
    value = value ^ lax.shift_right_logical(value, jnp.int32(16))
    value = value * jnp.int32(73244475)
    value = value ^ lax.shift_right_logical(value, jnp.int32(16))
    value = value * jnp.int32(73244475)
    value = value ^ lax.shift_right_logical(value, jnp.int32(16))
    return value


def keep_factor(seeds, first_unit):
    units = first_unit + jnp.arange(BS, dtype=jnp.int32)
    mixed = scramble(seeds[:, None] + units[None, :] * jnp.int32(668265261))
    kept = mixed & jnp.int32(7) != jnp.int32(0)
    return kept.astype(F32) * jnp.float32(8.0 / 7.0)


def gelu_parts(pre_act):
    coeff = math.sqrt(2.0 / math.pi)
    inner = coeff * (pre_act + 0.044715 * pre_act**3)
    tanh_val = jnp.tanh(inner)
    activation = 0.5 * pre_act * (1.0 + tanh_val)
    slope = 0.5 * (1.0 + tanh_val) + 0.5 * pre_act * (1.0 - tanh_val * tanh_val) * coeff * (
        1.0 + 3.0 * 0.044715 * pre_act * pre_act
    )
    return (activation, slope)


def dot(left, right, dims):
    return lax.dot_general(left, right, (dims, ((), ())), preferred_element_type=F32)


def slot(listed, count, first, at):
    number = first ^ at
    return listed[number], (number < listed[count]).astype(F32)


def block_of(picks, half, place):
    local = picks.shape[0] // 2
    rows = picks[:, place * BS : (place + 1) * BS].astype(F32)
    return rows[half * local : (half + 1) * local].astype(BF16)


def side_by_side(weights, slots):
    return jnp.concatenate([weights[0, j] for j in range(slots)], axis=1)


def stacked(weights, slots):
    return weights[0].reshape(slots * BS, BS)


def add_slots(slots, picks, pre, grad, masks_in, masks_out, firsts, seconds):
    local = picks.shape[0] // 2
    span = slots * BS
    for mask, first in zip(masks_in, firsts):
        rows = picks[:, mask * span : (mask + 1) * span].astype(F32)[:local].astype(BF16)
        pre += dot(rows, stacked(first, slots), ((1,), (0,)))
    for mask, second in zip(masks_out, seconds):
        rows = picks[:, mask * span : (mask + 1) * span].astype(F32)[local:].astype(BF16)
        grad += dot(rows, side_by_side(second, slots), ((1,), (1,)))
    return pre, grad


def select_kernel(slots, masks_in, masks_out, listed, tokens, *refs):
    *weights, picks, table, sums = refs
    first = lax.axis_index("dp") * slots
    local = sums.shape[0] // 2
    row = lax.broadcasted_iota(jnp.int32, table.shape, 0)
    lane = lax.broadcasted_iota(jnp.int32, table.shape, 1)
    entries = jnp.zeros(table.shape, jnp.int32)
    odd = lax.axis_index("mp") % 2
    count = picks.shape[1] // BS
    for place in range(count):
        mask = place // slots
        turned = (mirrored(mask, count // slots) - mask) * slots
        index, used = slot(listed, count, first, place + odd * turned)
        at = pl.ds(pl.multiple_of(index * BS, BS), BS)
        picks[:, place * BS : (place + 1) * BS] = (tokens[:, at].astype(F32) * used).astype(BF16)
        entry = jnp.where(row == 0, index, used.astype(jnp.int32))
        entries = jnp.where(lane == place, entry, entries)
    table[...] = entries
    zero = jnp.zeros((local, BS), F32)
    firsts, seconds = weights[: len(masks_in)], weights[len(masks_in) :]
    pre, grad = add_slots(slots, picks, zero, zero, masks_in, masks_out, firsts, seconds)
    sums[:local] = pre
    sums[local:] = grad


def partial_kernel(slots, masks_in, masks_out, picks, *refs):
    *weights, sums, out = refs
    local = picks.shape[0] // 2
    seconds, firsts = weights[: len(masks_out)], weights[len(masks_out) :]
    pre, grad = add_slots(slots, picks, sums[:local], sums[local:], masks_in, masks_out, firsts, seconds)
    out[:local] = pre
    out[local:] = grad


def bit_parity(number, size):
    return functools.reduce(lambda found, i: found ^ number >> i & 1, range(1, size.bit_length()), number & 1)


def place(acc, rows, entries, start, slots, mask):
    half = acc.shape[0]
    for j in range(slots):
        at = mask * slots + j
        index, used = entries[0, at], entries[1, at].astype(F32)
        block = rows[:, j * BS : (j + 1) * BS] * used
        acc[:, :, pl.ds(start + index, 1), :] = block.reshape(half, 2, 1, BS)


def activation_kernel(slots, early, late, picks, table, keep, sums, first, *refs):
    *seconds, hidden, out = refs
    local = keep.shape[0]
    out[...] = jnp.zeros_like(out)
    entries = table[...]
    pre, _ = add_slots(slots, picks, sums[:local], None, [late], [], [first], [])
    activation, slope = gelu_parts(pre)
    dropped = activation * keep[...]
    hidden[:local] = dropped
    hidden[local:] = keep[...] * slope
    for mask, second in zip(early, seconds):
        place(out, dot(dropped.astype(BF16), side_by_side(second, slots), ((1,), (0,))), entries, 0, slots, mask)


def hidden_kernel(slots, late, picks, table, sums, hidden, out, second, *refs):
    acc = refs[-1]
    firsts, (away, home, *rows) = refs[: late + 1], refs[late + 1 : -1]
    local = hidden.shape[0] // 2
    half, blocks = local // 2, out.shape[2]
    entries = table[...]
    _, grad = add_slots(slots, picks, None, sums[local:], [], [late], [], [second])
    dropped, grad_pre = hidden[:local], grad * hidden[local:]
    acc[:, :, :blocks] = out[...]
    acc[:, :, blocks:] = jnp.zeros_like(out)
    place(acc, dot(dropped.astype(BF16), side_by_side(second, slots), ((1,), (0,))), entries, 0, slots, late)
    for mask, first in enumerate(firsts):
        in_rows = dot(grad_pre.astype(BF16), stacked(first, slots), ((1,), (1,)))
        place(acc, in_rows, entries, blocks, slots, mask)
    odd = bit_parity(lax.axis_index("mp"), 2 * half)
    for i in range(half):
        even_row, odd_row = acc[i, bit_parity(i, half)], acc[i, 1 - bit_parity(i, half)]
        away[i] = jnp.where(odd == 1, even_row, odd_row).astype(BF16)
        home[i] = jnp.where(odd == 1, odd_row, even_row)
    both = jnp.concatenate([dropped, grad_pre], axis=0).astype(BF16)
    for mask, message in enumerate(rows):
        message[:, :BS] = both
        message[:, BS:] = picks[:, mask * slots * BS : (mask + 1) * slots * BS]


def all_rows(messages, half, place):
    return jnp.concatenate([block_of(message, half, place) for message in messages], axis=0)


def grad_kernel(slots, *refs):
    *messages, grad_in, grad_out, order = refs
    order[...] = jnp.zeros_like(order)
    dropped, grad_pre = all_rows(messages, 0, 0), all_rows(messages, 1, 0)
    for j in range(slots):
        grad_in[0, j] = dot(all_rows(messages, 0, 1 + j), grad_pre, ((0,), (0,)))
        grad_out[0, j] = dot(dropped, all_rows(messages, 1, 1 + j), ((0,), (0,)))


def last_kernel(blocks, kept, got, order, outputs, input_grad):
    for row in range(kept.shape[0]):
        total = kept[row] + got[row].astype(F32)
        for result, start in ((outputs, 0), (input_grad, blocks)):
            line = [total[start + i : start + i + 1] for i in range(blocks)]
            result[row : row + 1] = jnp.concatenate(line, axis=1).astype(BF16)


def call(kernel, n_vmem, out_shape, flops, nbytes, scalars=0, scratch=()):
    vmem = pl.BlockSpec(memory_space=pltpu.VMEM)
    head = [pl.BlockSpec(memory_space=pltpu.SMEM)] * scalars
    return pl.pallas_call(
        kernel,
        out_shape=out_shape,
        in_specs=head + [vmem] * n_vmem,
        out_specs=jax.tree.map(lambda _: vmem, out_shape),
        scratch_shapes=list(scratch),
        compiler_params=pltpu.CompilerParams(vmem_limit_bytes=VMEM_LIMIT),
        cost_estimate=pl.CostEstimate(flops=flops, bytes_accessed=nbytes, transcendentals=0),
    )


def flip(value, axis, size, mask):
    return lax.ppermute(value, axis, [(i, i ^ mask) for i in range(size)]) if mask else value


def mirrored(mask, n_dp):
    width = n_dp.bit_length() - 1
    return sum(1 << (width - 1 - i) for i in range(width) if mask >> i & 1)


def cross(value, n_dp, n_mp, mask):
    pairs = []
    for i in range(n_dp):
        for j in range(n_mp):
            other = i ^ (mirrored(mask, n_dp) if j % 2 else mask)
            pairs.append((i * n_mp + j, other * n_mp + j))
    return lax.ppermute(value, ("dp", "mp"), pairs)


def gather(values, held, n_dp, n_mp, orders):
    pieces = [{0: value} for value in values]
    for step, bits in enumerate(zip(*orders)):
        pieces = [
            {**parts, **{mask | bit: cross(part, n_dp, n_mp, bit) for mask, part in parts.items()}}
            for parts, bit in zip(pieces, bits)
        ]
        if step == 0:
            for parts, own in zip(pieces, held):
                parts[0] = own
    for parts, value in zip(pieces, values):
        parts[0] = value
        for mask in parts:
            parts[mask] = parts[mask].reshape(value.shape)
    return pieces


def exchange(messages, n_dp, n_mp, bits):
    for bit in bits:
        size = messages[0].shape[1]
        leaving = jnp.concatenate([message for mask, message in enumerate(messages) if mask & bit], axis=1)
        arrived = cross(leaving, n_dp, n_mp, bit)
        place = 0
        for mask in range(len(messages)):
            if mask & bit:
                messages[mask] = arrived[:, place * size : (place + 1) * size]
                place += 1
    return messages


def body(n_dp, n_mp, inputs, cotangent, w_in, w_out, block_index, block_count, drop_seeds):
    local, width = inputs.shape
    blocks = width // BS
    slots = w_in.shape[1]
    shape = jax.ShapeDtypeStruct
    piece_flops = 2 * local * slots * BS * BS
    piece_bytes = slots * BS * BS * 2

    bits = [1 << i for i in range(n_dp.bit_length() - 1)]
    firsts, seconds = gather([w_in, w_out], [w_in[0], w_out[0]], n_dp, n_mp, [bits, bits[::-1]])

    rank = lax.axis_index("mp")
    keep = keep_factor(drop_seeds, rank * BS)
    steps = [([0, bits[0]], [0, bits[-1]])]
    steps.append([[mask for mask in range(n_dp - 1) if mask not in done] for done in steps[0]])
    weights = [[firsts[m] for m in masks_in] + [seconds[m] for m in masks_out] for masks_in, masks_out in steps[:1]]
    weights.append([seconds[m] for m in steps[1][1]] + [firsts[m] for m in steps[1][0]])
    picks, table, sums = call(
        functools.partial(select_kernel, slots, *steps[0]),
        1 + len(weights[0]),
        [
            shape((2 * local, n_dp * slots * BS), BF16),
            shape((8, BS), jnp.int32),
            shape((2 * local, BS), F32),
        ],
        0,
        0,
        scalars=1,
    )(jnp.concatenate([block_index[0], block_count]), jnp.concatenate([inputs, cotangent]), *weights[0])
    sums = call(
        functools.partial(partial_kernel, slots, *steps[1]),
        2 + len(weights[1]),
        shape((2 * local, BS), F32),
        0,
        0,
    )(picks, *weights[1], sums)

    half = local // 2
    early, late = list(range(n_dp - 1)), n_dp - 1
    hidden, out = call(
        functools.partial(activation_kernel, slots, early, late),
        5 + len(early),
        [shape((2 * local, BS), F32), shape((half, 2, blocks, BS), F32)],
        0,
        0,
    )(picks, table, keep, sums, firsts[late], *[seconds[m] for m in early])
    away, home, *rows = call(
        functools.partial(hidden_kernel, slots, late),
        6 + n_dp,
        [shape((half, 2 * blocks, BS), BF16), shape((half, 2 * blocks, BS), F32)]
        + [shape((2 * local, (1 + slots) * BS), BF16)] * n_dp,
        (n_dp + 2) * piece_flops,
        (n_dp + 1) * piece_bytes,
        scratch=[pltpu.VMEM((half, 2, 2 * blocks, BS), F32)],
    )(picks, table, sums, hidden, out, seconds[late], *[firsts[m] for m in range(n_dp)])

    total = home + flip(away, "mp", n_mp, 1).astype(F32)
    messages = exchange(rows, n_dp, n_mp, bits)
    bit = n_mp // 2
    while bit > 1:
        mine_bit = (rank // bit) % 2
        cut = total.shape[0] // 2
        away = lax.dynamic_slice_in_dim(total, (1 - mine_bit) * cut, cut, 0)
        home = lax.dynamic_slice_in_dim(total, mine_bit * cut, cut, 0)
        got = flip(away.astype(BF16), "mp", n_mp, bit | 1)
        total = home + got.astype(F32)
        bit //= 2

    grad_shape = shape((1, slots, BS, BS), F32)
    grad_in, grad_out, order = call(
        functools.partial(grad_kernel, slots),
        n_dp,
        [grad_shape, grad_shape, shape((8, BS), F32)],
        2 * n_dp * piece_flops,
        4 * piece_bytes,
    )(*messages)
    done = home.shape[0]
    outputs, input_grad = call(
        functools.partial(last_kernel, blocks),
        3,
        [shape((done, width), BF16), shape((done, width), BF16)],
        done * 2 * width,
        done * 2 * width * 8,
    )(home, got, order)
    return (outputs, input_grad, grad_in, grad_out)


def solution(mesh):
    placed = (
        P("dp", None),
        P("dp", None),
        P("mp", "dp", None, None),
        P("mp", "dp", None, None),
        P("mp", None),
        P("mp"),
        P("dp"),
    )
    return jax.shard_map(
        functools.partial(body, mesh.shape["dp"], mesh.shape["mp"]),
        mesh=mesh,
        in_specs=placed,
        out_specs=(
            P(("dp", "mp"), None),
            P(("dp", "mp"), None),
            P("mp", "dp", None, None),
            P("mp", "dp", None, None),
        ),
        check_vma=False,
    )
```

```python
import functools
import math

import jax
import jax.numpy as jnp
from jax import lax
from jax.experimental import pallas as pl
from jax.experimental.pallas import tpu as pltpu
from jax.sharding import PartitionSpec as P

BS = 128
F32 = jnp.float32
BF16 = jnp.bfloat16
VMEM_LIMIT = 48 * 2**20


def scramble(value):
    value = value ^ lax.shift_right_logical(value, jnp.int32(16))
    value = value * jnp.int32(73244475)
    value = value ^ lax.shift_right_logical(value, jnp.int32(16))
    value = value * jnp.int32(73244475)
    value = value ^ lax.shift_right_logical(value, jnp.int32(16))
    return value


def keep_factor(seeds, first_unit):
    units = first_unit + jnp.arange(BS, dtype=jnp.int32)
    mixed = scramble(seeds[:, None] + units[None, :] * jnp.int32(668265261))
    kept = mixed & jnp.int32(7) != jnp.int32(0)
    return kept.astype(F32) * jnp.float32(8.0 / 7.0)


def gelu_parts(pre_act):
    coeff = math.sqrt(2.0 / math.pi)
    inner = coeff * (pre_act + 0.044715 * pre_act**3)
    tanh_val = jnp.tanh(inner)
    activation = 0.5 * pre_act * (1.0 + tanh_val)
    slope = 0.5 * (1.0 + tanh_val) + 0.5 * pre_act * (1.0 - tanh_val * tanh_val) * coeff * (
        1.0 + 3.0 * 0.044715 * pre_act * pre_act
    )
    return (activation, slope)


def dot(left, right, dims):
    return lax.dot_general(left, right, (dims, ((), ())), preferred_element_type=F32)


def slot(listed, count, first, at):
    number = first ^ at
    return listed[number], (number < listed[count]).astype(F32)


def block_of(picks, half, place):
    local = picks.shape[0] // 2
    rows = picks[:, place * BS : (place + 1) * BS].astype(F32)
    return rows[half * local : (half + 1) * local].astype(BF16)


def side_by_side(weights, slots):
    return jnp.concatenate([weights[0, j] for j in range(slots)], axis=1)


def stacked(weights, slots):
    return weights[0].reshape(slots * BS, BS)


def add_slots(slots, picks, pre, grad, masks_in, masks_out, firsts, seconds):
    local = picks.shape[0] // 2
    span = slots * BS
    for mask, first in zip(masks_in, firsts):
        rows = picks[:, mask * span : (mask + 1) * span].astype(F32)[:local].astype(BF16)
        pre += dot(rows, stacked(first, slots), ((1,), (0,)))
    for mask, second in zip(masks_out, seconds):
        rows = picks[:, mask * span : (mask + 1) * span].astype(F32)[local:].astype(BF16)
        grad += dot(rows, side_by_side(second, slots), ((1,), (1,)))
    return pre, grad


def select_kernel(slots, masks_in, masks_out, listed, tokens, *refs):
    *weights, picks, table, sums = refs
    first = lax.axis_index("dp") * slots
    local = sums.shape[0] // 2
    row = lax.broadcasted_iota(jnp.int32, table.shape, 0)
    lane = lax.broadcasted_iota(jnp.int32, table.shape, 1)
    entries = jnp.zeros(table.shape, jnp.int32)
    odd = lax.axis_index("mp") % 2
    count = picks.shape[1] // BS
    for place in range(count):
        mask = place // slots
        turned = (mirrored(mask, count // slots) - mask) * slots
        index, used = slot(listed, count, first, place + odd * turned)
        at = pl.ds(pl.multiple_of(index * BS, BS), BS)
        picks[:, place * BS : (place + 1) * BS] = (tokens[:, at].astype(F32) * used).astype(BF16)
        entry = jnp.where(row == 0, index, used.astype(jnp.int32))
        entries = jnp.where(lane == place, entry, entries)
    table[...] = entries
    zero = jnp.zeros((local, BS), F32)
    firsts, seconds = weights[: len(masks_in)], weights[len(masks_in) :]
    pre, grad = add_slots(slots, picks, zero, zero, masks_in, masks_out, firsts, seconds)
    sums[:local] = pre
    sums[local:] = grad


def partial_kernel(slots, masks_in, masks_out, picks, *refs):
    *weights, sums, out = refs
    local = picks.shape[0] // 2
    seconds, firsts = weights[: len(masks_out)], weights[len(masks_out) :]
    pre, grad = add_slots(slots, picks, sums[:local], sums[local:], masks_in, masks_out, firsts, seconds)
    out[:local] = pre
    out[local:] = grad


def bit_parity(number, size):
    return functools.reduce(lambda found, i: found ^ number >> i & 1, range(1, size.bit_length()), number & 1)


def place(acc, rows, entries, start, slots, mask):
    half = acc.shape[0]
    for j in range(slots):
        at = mask * slots + j
        index, used = entries[0, at], entries[1, at].astype(F32)
        block = rows[:, j * BS : (j + 1) * BS] * used
        acc[:, :, pl.ds(start + index, 1), :] = block.reshape(half, 2, 1, BS)


def activation_kernel(slots, early, late, picks, table, keep, sums, first, *refs):
    *seconds, hidden, out = refs
    local = keep.shape[0]
    out[...] = jnp.zeros_like(out)
    entries = table[...]
    pre, _ = add_slots(slots, picks, sums[:local], None, [late], [], [first], [])
    activation, slope = gelu_parts(pre)
    dropped = activation * keep[...]
    hidden[:local] = dropped
    hidden[local:] = keep[...] * slope
    for mask, second in zip(early, seconds):
        place(out, dot(dropped.astype(BF16), side_by_side(second, slots), ((1,), (0,))), entries, 0, slots, mask)


def hidden_kernel(slots, late, picks, table, sums, hidden, out, second, *refs):
    acc = refs[-1]
    firsts, (away, home, *rows) = refs[: late + 1], refs[late + 1 : -1]
    local = hidden.shape[0] // 2
    half, blocks = local // 2, out.shape[2]
    entries = table[...]
    _, grad = add_slots(slots, picks, None, sums[local:], [], [late], [], [second])
    dropped, grad_pre = hidden[:local], grad * hidden[local:]
    acc[:, :, :blocks] = out[...]
    acc[:, :, blocks:] = jnp.zeros_like(out)
    place(acc, dot(dropped.astype(BF16), side_by_side(second, slots), ((1,), (0,))), entries, 0, slots, late)
    for mask, first in enumerate(firsts):
        in_rows = dot(grad_pre.astype(BF16), stacked(first, slots), ((1,), (1,)))
        place(acc, in_rows, entries, blocks, slots, mask)
    odd = bit_parity(lax.axis_index("mp"), 2 * half)
    for i in range(half):
        even_row, odd_row = acc[i, bit_parity(i, half)], acc[i, 1 - bit_parity(i, half)]
        away[i] = jnp.where(odd == 1, even_row, odd_row).astype(BF16)
        home[i] = jnp.where(odd == 1, odd_row, even_row)
    both = jnp.concatenate([dropped, grad_pre], axis=0).astype(BF16)
    for mask, message in enumerate(rows):
        message[:, :BS] = both
        message[:, BS:] = picks[:, mask * slots * BS : (mask + 1) * slots * BS]


def all_rows(messages, half, place):
    return jnp.concatenate([block_of(message, half, place) for message in messages], axis=0)


def grad_kernel(slots, *refs):
    *messages, grad_in, grad_out, order = refs
    order[...] = jnp.zeros_like(order)
    dropped, grad_pre = all_rows(messages, 0, 0), all_rows(messages, 1, 0)
    for j in range(slots):
        grad_in[0, j] = dot(all_rows(messages, 0, 1 + j), grad_pre, ((0,), (0,)))
        grad_out[0, j] = dot(dropped, all_rows(messages, 1, 1 + j), ((0,), (0,)))


def last_kernel(blocks, kept, got, order, outputs, input_grad):
    for row in range(kept.shape[0]):
        total = kept[row] + got[row].astype(F32)
        for result, start in ((outputs, 0), (input_grad, blocks)):
            line = [total[start + i : start + i + 1] for i in range(blocks)]
            result[row : row + 1] = jnp.concatenate(line, axis=1).astype(BF16)


def call(kernel, n_vmem, out_shape, flops, nbytes, scalars=0, scratch=()):
    vmem = pl.BlockSpec(memory_space=pltpu.VMEM)
    head = [pl.BlockSpec(memory_space=pltpu.SMEM)] * scalars
    return pl.pallas_call(
        kernel,
        out_shape=out_shape,
        in_specs=head + [vmem] * n_vmem,
        out_specs=jax.tree.map(lambda _: vmem, out_shape),
        scratch_shapes=list(scratch),
        compiler_params=pltpu.CompilerParams(vmem_limit_bytes=VMEM_LIMIT),
        cost_estimate=pl.CostEstimate(flops=flops, bytes_accessed=nbytes, transcendentals=0),
    )


def flip(value, axis, size, mask):
    return lax.ppermute(value, axis, [(i, i ^ mask) for i in range(size)]) if mask else value


def mirrored(mask, n_dp):
    width = n_dp.bit_length() - 1
    return sum(1 << (width - 1 - i) for i in range(width) if mask >> i & 1)


def cross(value, n_dp, n_mp, mask):
    pairs = []
    for i in range(n_dp):
        for j in range(n_mp):
            other = i ^ (mirrored(mask, n_dp) if j % 2 else mask)
            pairs.append((i * n_mp + j, other * n_mp + j))
    return lax.ppermute(value, ("dp", "mp"), pairs)


def gather(values, held, n_dp, n_mp, orders):
    pieces = [{0: value} for value in values]
    for step, bits in enumerate(zip(*orders)):
        pieces = [
            {**parts, **{mask | bit: cross(part, n_dp, n_mp, bit) for mask, part in parts.items()}}
            for parts, bit in zip(pieces, bits)
        ]
        if step == 0:
            for parts, own in zip(pieces, held):
                parts[0] = own
    for parts, value in zip(pieces, values):
        parts[0] = value
        for mask in parts:
            parts[mask] = parts[mask].reshape(value.shape)
    return pieces


def exchange(messages, n_dp, n_mp, bits):
    for bit in bits:
        size = messages[0].shape[1]
        leaving = jnp.concatenate([message for mask, message in enumerate(messages) if mask & bit], axis=1)
        arrived = cross(leaving, n_dp, n_mp, bit)
        place = 0
        for mask in range(len(messages)):
            if mask & bit:
                messages[mask] = arrived[:, place * size : (place + 1) * size]
                place += 1
    return messages


def body(n_dp, n_mp, inputs, cotangent, w_in, w_out, block_index, block_count, drop_seeds):
    local, width = inputs.shape
    blocks = width // BS
    slots = w_in.shape[1]
    shape = jax.ShapeDtypeStruct
    piece_flops = 2 * local * slots * BS * BS
    piece_bytes = slots * BS * BS * 2

    bits = [1 << i for i in range(n_dp.bit_length() - 1)]
    tokens = jnp.concatenate([inputs, cotangent])
    *held, tokens = lax.optimization_barrier((w_in[0], w_out[0], tokens))
    firsts, seconds = gather([w_in, w_out], held, n_dp, n_mp, [bits, bits[::-1]])

    rank = lax.axis_index("mp")
    keep = keep_factor(drop_seeds, rank * BS)
    steps = [([0, bits[0]], [0, bits[-1]])]
    steps.append([[mask for mask in range(n_dp - 1) if mask not in done] for done in steps[0]])
    weights = [[firsts[m] for m in masks_in] + [seconds[m] for m in masks_out] for masks_in, masks_out in steps[:1]]
    weights.append([seconds[m] for m in steps[1][1]] + [firsts[m] for m in steps[1][0]])
    picks, table, sums = call(
        functools.partial(select_kernel, slots, *steps[0]),
        1 + len(weights[0]),
        [
            shape((2 * local, n_dp * slots * BS), BF16),
            shape((8, BS), jnp.int32),
            shape((2 * local, BS), F32),
        ],
        0,
        0,
        scalars=1,
    )(jnp.concatenate([block_index[0], block_count]), tokens, *weights[0])
    sums = call(
        functools.partial(partial_kernel, slots, *steps[1]),
        2 + len(weights[1]),
        shape((2 * local, BS), F32),
        0,
        0,
    )(picks, *weights[1], sums)

    half = local // 2
    early, late = list(range(n_dp - 1)), n_dp - 1
    hidden, out = call(
        functools.partial(activation_kernel, slots, early, late),
        5 + len(early),
        [shape((2 * local, BS), F32), shape((half, 2, blocks, BS), F32)],
        0,
        0,
    )(picks, table, keep, sums, firsts[late], *[seconds[m] for m in early])
    away, home, *rows = call(
        functools.partial(hidden_kernel, slots, late),
        6 + n_dp,
        [shape((half, 2 * blocks, BS), BF16), shape((half, 2 * blocks, BS), F32)]
        + [shape((2 * local, (1 + slots) * BS), BF16)] * n_dp,
        (n_dp + 2) * piece_flops,
        (n_dp + 1) * piece_bytes,
        scratch=[pltpu.VMEM((half, 2, 2 * blocks, BS), F32)],
    )(picks, table, sums, hidden, out, seconds[late], *[firsts[m] for m in range(n_dp)])

    total = home + flip(away, "mp", n_mp, 1).astype(F32)
    messages = exchange(rows, n_dp, n_mp, bits)
    bit = n_mp // 2
    while bit > 1:
        mine_bit = (rank // bit) % 2
        cut = total.shape[0] // 2
        away = lax.dynamic_slice_in_dim(total, (1 - mine_bit) * cut, cut, 0)
        home = lax.dynamic_slice_in_dim(total, mine_bit * cut, cut, 0)
        got = flip(away.astype(BF16), "mp", n_mp, bit | 1)
        total = home + got.astype(F32)
        bit //= 2

    grad_shape = shape((1, slots, BS, BS), F32)
    grad_in, grad_out, order = call(
        functools.partial(grad_kernel, slots),
        n_dp,
        [grad_shape, grad_shape, shape((8, BS), F32)],
        2 * n_dp * piece_flops,
        4 * piece_bytes,
    )(*messages)
    done = home.shape[0]
    outputs, input_grad = call(
        functools.partial(last_kernel, blocks),
        3,
        [shape((done, width), BF16), shape((done, width), BF16)],
        done * 2 * width,
        done * 2 * width * 8,
    )(home, got, order)
    return (outputs, input_grad, grad_in, grad_out)


def solution(mesh):
    placed = (
        P("dp", None),
        P("dp", None),
        P("mp", "dp", None, None),
        P("mp", "dp", None, None),
        P("mp", None),
        P("mp"),
        P("dp"),
    )
    return jax.shard_map(
        functools.partial(body, mesh.shape["dp"], mesh.shape["mp"]),
        mesh=mesh,
        in_specs=placed,
        out_specs=(
            P(("dp", "mp"), None),
            P(("dp", "mp"), None),
            P("mp", "dp", None, None),
            P("mp", "dp", None, None),
        ),
        check_vma=False,
    )
```

```python
import functools
import math

import jax
import jax.numpy as jnp
from jax import lax
from jax.experimental import pallas as pl
from jax.experimental.pallas import tpu as pltpu
from jax.sharding import PartitionSpec as P

BS = 128
F32 = jnp.float32
BF16 = jnp.bfloat16
VMEM_LIMIT = 48 * 2**20


def scramble(value):
    value = value ^ lax.shift_right_logical(value, jnp.int32(16))
    value = value * jnp.int32(73244475)
    value = value ^ lax.shift_right_logical(value, jnp.int32(16))
    value = value * jnp.int32(73244475)
    value = value ^ lax.shift_right_logical(value, jnp.int32(16))
    return value


def keep_factor(seeds, first_unit):
    units = first_unit + jnp.arange(BS, dtype=jnp.int32)
    mixed = scramble(seeds[:, None] + units[None, :] * jnp.int32(668265261))
    kept = mixed & jnp.int32(7) != jnp.int32(0)
    return kept.astype(F32) * jnp.float32(8.0 / 7.0)


def gelu_parts(pre_act):
    coeff = math.sqrt(2.0 / math.pi)
    inner = coeff * (pre_act + 0.044715 * pre_act**3)
    tanh_val = jnp.tanh(inner)
    activation = 0.5 * pre_act * (1.0 + tanh_val)
    slope = 0.5 * (1.0 + tanh_val) + 0.5 * pre_act * (1.0 - tanh_val * tanh_val) * coeff * (
        1.0 + 3.0 * 0.044715 * pre_act * pre_act
    )
    return (activation, slope)


def dot(left, right, dims):
    return lax.dot_general(left, right, (dims, ((), ())), preferred_element_type=F32)


def slot(listed, count, first, at):
    number = first ^ at
    return listed[number], (number < listed[count]).astype(F32)


def block_of(picks, half, place):
    local = picks.shape[0] // 2
    rows = picks[:, place * BS : (place + 1) * BS].astype(F32)
    return rows[half * local : (half + 1) * local].astype(BF16)


def side_by_side(weights, slots):
    return jnp.concatenate([weights[0, j] for j in range(slots)], axis=1)


def stacked(weights, slots):
    return weights[0].reshape(slots * BS, BS)


def add_slots(slots, picks, pre, grad, masks_in, masks_out, firsts, seconds):
    local = picks.shape[0] // 2
    span = slots * BS
    for mask, first in zip(masks_in, firsts):
        rows = picks[:, mask * span : (mask + 1) * span].astype(F32)[:local].astype(BF16)
        pre += dot(rows, stacked(first, slots), ((1,), (0,)))
    for mask, second in zip(masks_out, seconds):
        rows = picks[:, mask * span : (mask + 1) * span].astype(F32)[local:].astype(BF16)
        grad += dot(rows, side_by_side(second, slots), ((1,), (1,)))
    return pre, grad


def select_kernel(slots, masks_in, masks_out, listed, tokens, *refs):
    *weights, picks, table, sums = refs
    first = lax.axis_index("dp") * slots
    local = sums.shape[0] // 2
    row = lax.broadcasted_iota(jnp.int32, table.shape, 0)
    lane = lax.broadcasted_iota(jnp.int32, table.shape, 1)
    entries = jnp.zeros(table.shape, jnp.int32)
    odd = lax.axis_index("mp") % 2
    count = picks.shape[1] // BS
    for place in range(count):
        mask = place // slots
        turned = (mirrored(mask, count // slots) - mask) * slots
        index, used = slot(listed, count, first, place + odd * turned)
        at = pl.ds(pl.multiple_of(index * BS, BS), BS)
        picks[:, place * BS : (place + 1) * BS] = (tokens[:, at].astype(F32) * used).astype(BF16)
        entry = jnp.where(row == 0, index, used.astype(jnp.int32))
        entries = jnp.where(lane == place, entry, entries)
    table[...] = entries
    zero = jnp.zeros((local, BS), F32)
    firsts, seconds = weights[: len(masks_in)], weights[len(masks_in) :]
    pre, grad = add_slots(slots, picks, zero, zero, masks_in, masks_out, firsts, seconds)
    sums[:local] = pre
    sums[local:] = grad


def partial_kernel(slots, masks_in, masks_out, picks, *refs):
    *weights, sums, out = refs
    local = picks.shape[0] // 2
    seconds, firsts = weights[: len(masks_out)], weights[len(masks_out) :]
    pre, grad = add_slots(slots, picks, sums[:local], sums[local:], masks_in, masks_out, firsts, seconds)
    out[:local] = pre
    out[local:] = grad


def bit_parity(number, size):
    return functools.reduce(lambda found, i: found ^ number >> i & 1, range(1, size.bit_length()), number & 1)


def hidden_kernel(slots, blocks, masks_in, masks_out, late, picks, table, keep, sums, *refs):
    count = len(masks_in)
    firsts = dict(zip(masks_in, refs[:count]))
    seconds = dict(zip(masks_out, refs[count : 2 * count]))
    away, home, *rows = refs[2 * count : -1]
    acc = refs[-1]
    local = keep.shape[0]
    half = local // 2
    acc[...] = jnp.zeros_like(acc)
    entries = table[...]
    pre, grad = add_slots(
        slots, picks, sums[:local], sums[local:], late, late, [firsts[m] for m in late], [seconds[m] for m in late]
    )
    activation, slope = gelu_parts(pre)
    dropped_full = activation * keep[...]
    grad_full = grad * keep[...] * slope
    dropped, grad_pre = dropped_full.astype(BF16), grad_full.astype(BF16)
    for mask in range(count):
        out_row = dot(dropped, side_by_side(seconds[mask], slots), ((1,), (0,)))
        in_row = dot(grad_pre, stacked(firsts[mask], slots), ((1,), (1,)))
        for j in range(slots):
            at = mask * slots + j
            index, used = entries[0, at], entries[1, at].astype(F32)
            cut = slice(j * BS, (j + 1) * BS)
            acc[:, :, pl.ds(index, 1), :] = (out_row[:, cut] * used).reshape(half, 2, 1, BS)
            acc[:, :, pl.ds(blocks + index, 1), :] = (in_row[:, cut] * used).reshape(half, 2, 1, BS)
    odd = bit_parity(lax.axis_index("mp"), 2 * half)
    for i in range(half):
        even_row, odd_row = acc[i, bit_parity(i, half)], acc[i, 1 - bit_parity(i, half)]
        away[i] = jnp.where(odd == 1, even_row, odd_row).astype(BF16)
        home[i] = jnp.where(odd == 1, odd_row, even_row)
    hidden = jnp.concatenate([dropped_full, grad_full], axis=0).astype(BF16)
    for mask, message in enumerate(rows):
        message[:, :BS] = hidden
        message[:, BS:] = picks[:, mask * slots * BS : (mask + 1) * slots * BS]


def all_rows(messages, half, place):
    return jnp.concatenate([block_of(message, half, place) for message in messages], axis=0)


def grad_kernel(slots, *refs):
    *messages, grad_in, grad_out, order = refs
    order[...] = jnp.zeros_like(order)
    dropped, grad_pre = all_rows(messages, 0, 0), all_rows(messages, 1, 0)
    for j in range(slots):
        grad_in[0, j] = dot(all_rows(messages, 0, 1 + j), grad_pre, ((0,), (0,)))
        grad_out[0, j] = dot(dropped, all_rows(messages, 1, 1 + j), ((0,), (0,)))


def last_kernel(blocks, kept, got, order, outputs, input_grad):
    for row in range(kept.shape[0]):
        total = kept[row] + got[row].astype(F32)
        for result, start in ((outputs, 0), (input_grad, blocks)):
            line = [total[start + i : start + i + 1] for i in range(blocks)]
            result[row : row + 1] = jnp.concatenate(line, axis=1).astype(BF16)


def call(kernel, n_vmem, out_shape, flops, nbytes, scalars=0, scratch=()):
    vmem = pl.BlockSpec(memory_space=pltpu.VMEM)
    head = [pl.BlockSpec(memory_space=pltpu.SMEM)] * scalars
    return pl.pallas_call(
        kernel,
        out_shape=out_shape,
        in_specs=head + [vmem] * n_vmem,
        out_specs=jax.tree.map(lambda _: vmem, out_shape),
        scratch_shapes=list(scratch),
        compiler_params=pltpu.CompilerParams(vmem_limit_bytes=VMEM_LIMIT),
        cost_estimate=pl.CostEstimate(flops=flops, bytes_accessed=nbytes, transcendentals=0),
    )


def flip(value, axis, size, mask):
    return lax.ppermute(value, axis, [(i, i ^ mask) for i in range(size)]) if mask else value


def mirrored(mask, n_dp):
    width = n_dp.bit_length() - 1
    return sum(1 << (width - 1 - i) for i in range(width) if mask >> i & 1)


def cross(value, n_dp, n_mp, mask):
    pairs = []
    for i in range(n_dp):
        for j in range(n_mp):
            other = i ^ (mirrored(mask, n_dp) if j % 2 else mask)
            pairs.append((i * n_mp + j, other * n_mp + j))
    return lax.ppermute(value, ("dp", "mp"), pairs)


def gather(values, held, n_dp, n_mp, orders):
    pieces = [{0: value} for value in values]
    for step, bits in enumerate(zip(*orders)):
        pieces = [
            {**parts, **{mask | bit: cross(part, n_dp, n_mp, bit) for mask, part in parts.items()}}
            for parts, bit in zip(pieces, bits)
        ]
        if step == 0:
            for parts, own in zip(pieces, held):
                parts[0] = own
    for parts, value in zip(pieces, values):
        parts[0] = value
        for mask in parts:
            parts[mask] = parts[mask].reshape(value.shape)
    return pieces


def exchange(messages, n_dp, n_mp, bits):
    for bit in bits:
        size = messages[0].shape[1]
        leaving = jnp.concatenate([message for mask, message in enumerate(messages) if mask & bit], axis=1)
        arrived = cross(leaving, n_dp, n_mp, bit)
        place = 0
        for mask in range(len(messages)):
            if mask & bit:
                messages[mask] = arrived[:, place * size : (place + 1) * size]
                place += 1
    return messages


def body(n_dp, n_mp, inputs, cotangent, w_in, w_out, block_index, block_count, drop_seeds):
    local, width = inputs.shape
    blocks = width // BS
    slots = w_in.shape[1]
    shape = jax.ShapeDtypeStruct
    piece_flops = 2 * local * slots * BS * BS
    piece_bytes = slots * BS * BS * 2

    bits = [1 << i for i in range(n_dp.bit_length() - 1)]
    tokens = jnp.concatenate([inputs, cotangent])
    *held, tokens = lax.optimization_barrier((w_in[0], w_out[0], tokens))
    firsts, seconds = gather([w_in, w_out], held, n_dp, n_mp, [bits, bits[::-1]])

    rank = lax.axis_index("mp")
    keep = keep_factor(drop_seeds, rank * BS)
    steps = [([0, bits[0]], [0, bits[-1]])]
    late = [n_dp - 1]
    steps.append([[mask for mask in range(n_dp - 1) if mask not in done] for done in steps[0]])
    weights = [[firsts[m] for m in masks_in] + [seconds[m] for m in masks_out] for masks_in, masks_out in steps[:1]]
    weights.append([seconds[m] for m in steps[1][1]] + [firsts[m] for m in steps[1][0]])
    picks, table, sums = call(
        functools.partial(select_kernel, slots, *steps[0]),
        1 + len(weights[0]),
        [
            shape((2 * local, n_dp * slots * BS), BF16),
            shape((8, BS), jnp.int32),
            shape((2 * local, BS), F32),
        ],
        0,
        0,
        scalars=1,
    )(jnp.concatenate([block_index[0], block_count]), tokens, *weights[0])
    sums = call(
        functools.partial(partial_kernel, slots, *steps[1]),
        2 + len(weights[1]),
        shape((2 * local, BS), F32),
        0,
        0,
    )(picks, *weights[1], sums)

    half = local // 2
    masks_in, masks_out = sorted(firsts), sorted(seconds)
    away, home, *rows = call(
        functools.partial(hidden_kernel, slots, blocks, masks_in, masks_out, late),
        4 + 2 * n_dp,
        [shape((half, 2 * blocks, BS), BF16), shape((half, 2 * blocks, BS), F32)]
        + [shape((2 * local, (1 + slots) * BS), BF16)] * n_dp,
        (2 * n_dp + 2) * piece_flops,
        2 * n_dp * piece_bytes,
        scratch=[pltpu.VMEM((half, 2, 2 * blocks, BS), F32)],
    )(picks, table, keep, sums, *[firsts[m] for m in masks_in], *[seconds[m] for m in masks_out])

    total = home + flip(away, "mp", n_mp, 1).astype(F32)
    messages = exchange(rows, n_dp, n_mp, bits)
    bit = n_mp // 2
    while bit > 1:
        mine_bit = (rank // bit) % 2
        cut = total.shape[0] // 2
        away = lax.dynamic_slice_in_dim(total, (1 - mine_bit) * cut, cut, 0)
        home = lax.dynamic_slice_in_dim(total, mine_bit * cut, cut, 0)
        got = flip(away.astype(BF16), "mp", n_mp, bit | 1)
        total = home + got.astype(F32)
        bit //= 2

    grad_shape = shape((1, slots, BS, BS), F32)
    grad_in, grad_out, order = call(
        functools.partial(grad_kernel, slots),
        n_dp,
        [grad_shape, grad_shape, shape((8, BS), F32)],
        2 * n_dp * piece_flops,
        4 * piece_bytes,
    )(*messages)
    done = home.shape[0]
    outputs, input_grad = call(
        functools.partial(last_kernel, blocks),
        3,
        [shape((done, width), BF16), shape((done, width), BF16)],
        done * 2 * width,
        done * 2 * width * 8,
    )(home, got, order)
    return (outputs, input_grad, grad_in, grad_out)


def solution(mesh):
    placed = (
        P("dp", None),
        P("dp", None),
        P("mp", "dp", None, None),
        P("mp", "dp", None, None),
        P("mp", None),
        P("mp"),
        P("dp"),
    )
    return jax.shard_map(
        functools.partial(body, mesh.shape["dp"], mesh.shape["mp"]),
        mesh=mesh,
        in_specs=placed,
        out_specs=(
            P(("dp", "mp"), None),
            P(("dp", "mp"), None),
            P("mp", "dp", None, None),
            P("mp", "dp", None, None),
        ),
        check_vma=False,
    )
```
